256 devices in a mesh: depth: 2 (over core), row: 8 (over z), col: 16 (over y, x).
Axes of the slice: x: 4, y: 4, z: 8, core: 2. Of those that a mesh axis runs over, the one named last changes fastest.
Arguments:
- tokens: bfloat16 [2048, 6144], P(('depth', 'row'), 'col'), may hold values from -6 to 6
- weight: bfloat16 [6144, 24576], P('col', 'row'), may hold values from -0.078125 to 0.078125
- cotangent: bfloat16 [2048, 24576], P(('depth', 'col'), 'row'), may hold values from -6 to 6
Outputs:
- activated: bfloat16 [2048, 24576], P(('depth', 'col'), 'row')
- grad_tokens: bfloat16 [2048, 6144], P(('depth', 'row'), 'col')
- grad_weight: bfloat16 [6144, 24576], P('col', 'row')
The draws below stay inside these ranges and needn't reach their ends.
All inputs are finite; a program needn't handle non-finite values.
Results may differ from the reference program's by a relative error of at most 0.022.
Values may be sent and summed in bfloat16 or wider, within the bound.
A program may use at most 128 MiB of HBM per device.

```python
import math
import jax
import jax.numpy as jnp
from jax import lax

D = 6144
F = 24576
TOKENS = 2048
N_COL = 16


def with_spikes(array, key, source, target, parts, factor):
    def block_of(axis_at):
        return (jnp.arange(array.shape[axis_at]) // (array.shape[axis_at] // parts)).reshape((-1,) + (1,) * (array.ndim - 1 - axis_at))

    one_side = jax.random.permutation(key, parts)[block_of(target)]
    other_side = (block_of(target) + parts // 2) % parts
    return jnp.where((block_of(source) == one_side) | (block_of(source) == other_side), factor * array, array)


def block_levels(stream_key, dims, shards, least, high):
    gain = 1.0
    for position, shards_of in shards:
        draws = jax.random.uniform(jax.random.fold_in(jax.random.fold_in(stream_key, 6), position), (shards_of,), jnp.float32, least / len(shards), high / len(shards))
        gain = gain * jnp.repeat(jnp.exp(draws), dims[position] // shards_of).reshape((-1,) + (1,) * (len(dims) - 1 - position))
    return gain


def gaussian(key, extent, deviation, bound, split=(), held_as=jnp.bfloat16):
    level = block_levels(key, extent, split, -0.22, 0.18) if split else 1.0
    drawn = jax.random.normal(key, extent, jnp.float32) * deviation * level
    return jnp.minimum(jnp.maximum(drawn, -bound), bound).astype(held_as)


def heavy_noise(own_key, extent, scale, bound, cuts, heavy, held_as=jnp.bfloat16):
    entries = scale * jax.random.normal(own_key, extent, jnp.float32)
    if cuts:
        entries = entries * block_levels(own_key, extent, cuts, -0.22, 0.18)
    return jnp.clip(with_spikes(entries, jax.random.fold_in(own_key, 3), *heavy), -bound, bound).astype(held_as)


def setup_inputs(seed: int = 0) -> dict:
    key_of = jax.random.split(jax.random.key(seed), 4)
    tokens = heavy_noise(key_of[0], (TOKENS, D), 1.0, 6.0, ((0, 16), (1, 16)), (1, 0, 16, 2.0))
    weight = gaussian(key_of[1], (D, F), D ** -0.5, 0.078125, ((0, 16), (1, 8)))
    cotangent = heavy_noise(key_of[2], (TOKENS, F), 1.0, 6.0, ((0, 32), (1, 8)), (1, 0, 32, 2.75))
    return {"tokens": tokens, "weight": weight, "cotangent": cotangent}


def reference(tokens, weight, cotangent):
    width = D // N_COL

    def add_block(index, total):
        start = (index * width).astype(jnp.int32)
        rows = lax.dynamic_slice_in_dim(tokens, start, width, 1)
        block = lax.dynamic_slice_in_dim(weight, start, width, 0)
        term = jnp.dot(rows, block, preferred_element_type=jnp.float32).astype(jnp.bfloat16)
        return total + term.astype(jnp.float32)
    hidden = lax.fori_loop(jnp.int32(0), jnp.int32(N_COL), add_block, jnp.zeros((tokens.shape[0], weight.shape[1]), jnp.float32))
    cdf = 0.5 * (1.0 + jax.scipy.special.erf(hidden * (1.0 / math.sqrt(2.0))))
    density = jnp.exp(-0.5 * hidden * hidden) * (1.0 / math.sqrt(2.0 * math.pi))
    activated = (hidden * cdf).astype(jnp.bfloat16)
    grad_hidden = (cotangent.astype(jnp.float32) * (cdf + hidden * density)).astype(jnp.bfloat16)
    grad_tokens = lax.dot_general(grad_hidden, weight, (((1,), (1,)), ((), ())), preferred_element_type=jnp.float32).astype(jnp.bfloat16)
    grad_weight = lax.dot_general(tokens, grad_hidden, (((0,), (0,)), ((), ())), preferred_element_type=jnp.float32).astype(jnp.bfloat16)
    return (activated, grad_tokens, grad_weight)
```

```python
import functools
import math

import jax
import jax.numpy as jnp
from jax import lax
from jax.experimental import pallas as pl
from jax.experimental.pallas import tpu as pltpu
from jax.sharding import PartitionSpec as P

MESH = pl.DeviceIdType.MESH
NCH = 2
SIDE = 4
ROWS = 8
BF16 = jnp.bfloat16
F32 = jnp.float32


def gelu_parts(hidden):
    cdf = 0.5 * (1.0 + lax.erf(hidden * (1.0 / math.sqrt(2.0))))
    density = jnp.exp(-0.5 * hidden * hidden) * (1.0 / math.sqrt(2.0 * math.pi))
    return (cdf, density)


def schedule():
    tasks = [("I", 0, j) for j in (2, 1, 3, 0)]
    for n in range(NCH):
        more = n + 1 < NCH
        tasks += [("F", n, 2), ("F", n, 1), ("D", n, 2), ("F", n, 3), ("D", n, 1), ("F", n, 0)]
        if more:
            tasks += [("I", n + 1, 2), ("D", n, 3), ("I", n + 1, 1), ("D", n, 0)]
            tasks += [("I", n + 1, 3), ("F2", n, 0), ("I", n + 1, 0), ("D2", n, 0)]
        else:
            tasks += [("D", n, 3), ("D", n, 0), ("F2", n, 0), ("D2", n, 0)]
    for n in range(NCH):
        tasks += [("B", n, 0), ("A1", n, 0), ("B", n, 1), ("B", n, 3), ("A2", n, 0), ("C", n, 0)]
        tasks += [("B", n, 2), ("C", n, 1), ("C", n, 3), ("C", n, 2)]
    return tasks


def kernel(
    tok_hbm, w_hbm, cot_hbm, act_hbm, own_hbm, other_hbm, gt_hbm,
    w, cot, act, tok, tok_t, part, f1, r1, s, f2, r2, g, gw, gwb, gt, zsend, zrecv,
    local_sem, out_sem, z_send, z_recv, send, f1_sem, r1_sem, f2_sem, r2_sem, g_sem,
    dep_send, dep_recv, zs_send, zs_recv,
):
    fh = part.shape[-1]
    half = 32
    depth, row, col = (lax.axis_index(a) for a in ("depth", "row", "col"))
    yx = (col // SIDE, col % SIDE)
    lo, hi = pl.ds(0, half), pl.ds(half, half)

    loads = [
        pltpu.make_async_copy(tok_hbm, tok.at[0, pl.ds(2 * row, 2)], local_sem.at[0]),
        pltpu.make_async_copy(w_hbm, w, local_sem.at[1]),
        pltpu.make_async_copy(cot_hbm, cot, local_sem.at[2]),
    ]
    for load in loads:
        load.start()

    def grid_device(axis, delta):
        at = list(yx)
        at[axis] = (at[axis] + delta + SIDE) % SIDE
        return {"col": at[0] * SIDE + at[1]}

    def row_device(delta):
        return {"row": (row + delta + ROWS) % ROWS}

    other = {"depth": 1 - depth}

    barrier = pltpu.get_barrier_semaphore()
    peers = [row_device(d) for d in range(1, ROWS)]
    peers += [grid_device(axis, delta) for axis in (0, 1) for delta in (1, -1)]
    peers += [other]
    for peer in peers:
        pl.semaphore_signal(barrier, inc=1, device_id=peer, device_id_type=MESH)
    pl.semaphore_wait(barrier, len(peers))

    def remote(src, dst, ssem, rsem, device):
        return pltpu.make_async_remote_copy(
            src_ref=src, dst_ref=dst, send_sem=ssem, recv_sem=rsem,
            device_id=device, device_id_type=MESH,
        )

    def push(src, dst, ssem, rsem, device):
        remote(src, dst, ssem, rsem, device).start()

    def arrived(ref, rsem):
        remote(ref, ref, send.at[0, 0, 0], rsem, other).wait_recv()

    def sent(ref, ssem):
        remote(ref, ref, ssem, f2_sem.at[0, 0], other).wait_send()

    def rows_of(delta):
        return 2 * ((row + delta + ROWS) % ROWS)

    def two(delta):
        return tok.at[0, pl.ds(rows_of(delta), 2)]

    gt[...] = jnp.zeros_like(gt)
    loads[0].wait()
    push(two(0), two(0), z_send.at[0], z_recv.at[0], row_device(1))
    push(two(0), two(0), z_send.at[1], z_recv.at[1], row_device(-1))
    for step in (1, 2, 3):
        arrived(two(-step), z_recv.at[2 * step - 2])
        if step < 3:
            src = two(-step)
        else:
            src = tok.at[0, rows_of(-step)]
        push(src, src, z_send.at[2 * step], z_recv.at[2 * step if step < 3 else 6], row_device(1))
        arrived(two(step), z_recv.at[2 * step - 1])
        if step < 3:
            src = two(step)
        else:
            src = tok.at[0, rows_of(step) + 1]
        push(src, src, z_send.at[2 * step + 1], z_recv.at[2 * step + 1 if step < 3 else 7], row_device(-1))
    arrived(tok.at[0, rows_of(4)], z_recv.at[6])
    arrived(tok.at[0, rows_of(4) + 1], z_recv.at[7])
    for at_y in range(SIDE):
        for at_x in range(SIDE):
            tok[1, at_x * SIDE + at_y] = tok[0, at_y * SIDE + at_x]
    loads[1].wait()

    def transposes():
        for h in range(2):
            for at in range(SIDE):
                tok_t[h, at] = tok[h, pl.ds(SIDE * at, SIDE)].reshape(256, 384).T

    def ring(h):
        axis_a, axis_b = (1, 0) if h == 0 else (0, 1)
        return axis_a, axis_b, yx[axis_a], yx[axis_b]

    def slot(h, j, i):
        _, _, a, b = ring(h)
        return ((b + j) % SIDE) * SIDE + (a + i) % SIDE

    def columns(n, h):
        return pl.ds((2 * n + h) * fh, fh)

    def group(h, j):
        _, _, _, b = ring(h)
        return (b + j) % SIDE

    def task_i(n, h, j):
        axis_a = ring(h)[0]
        four = pl.ds(SIDE * group(h, j), SIDE)
        x = tok[h, four].reshape(256, 384)
        y = jnp.dot(x, w[:, columns(n, h)], preferred_element_type=F32).astype(BF16)
        part[n, h, four] = y.reshape(SIDE, 64, fh)
        right, left = grid_device(axis_a, 1), grid_device(axis_a, -1)
        ssem = send.at[n, h, 0]
        far = part.at[n, h, slot(h, j, 2)]
        push(far.at[lo], f1.at[n, h, j, 0], ssem, f1_sem.at[n, h, j], right)
        push(far.at[hi], f1.at[n, h, j, 1], ssem, f1_sem.at[n, h, j], left)
        push(part.at[n, h, slot(h, j, 1), hi], r1.at[n, h, j, 0, hi], ssem, r1_sem.at[n, h, j], right)
        push(part.at[n, h, slot(h, j, 3), lo], r1.at[n, h, j, 1, lo], ssem, r1_sem.at[n, h, j], left)

    def task_f(n, h, j):
        axis_a = ring(h)[0]
        right, left = grid_device(axis_a, 1), grid_device(axis_a, -1)
        ssem = send.at[n, h, 1]
        arrived(f1.at[n, h, j], f1_sem.at[n, h, j])
        f1[n, h, j, 0] = (f1[n, h, j, 0].astype(F32) + part[n, h, slot(h, j, 1), lo].astype(F32)).astype(BF16)
        push(f1.at[n, h, j, 0], r1.at[n, h, j, 0, lo], ssem, r1_sem.at[n, h, j], right)
        f1[n, h, j, 1] = (f1[n, h, j, 1].astype(F32) + part[n, h, slot(h, j, 3), hi].astype(F32)).astype(BF16)
        push(f1.at[n, h, j, 1], r1.at[n, h, j, 1, hi], ssem, r1_sem.at[n, h, j], left)

    def task_d(n, h, j):
        axis_b = ring(h)[1]
        right, left = grid_device(axis_b, 1), grid_device(axis_b, -1)
        ssem = send.at[n, h, 2]
        arrived(r1.at[n, h, j], r1_sem.at[n, h, j])
        total = part[n, h, slot(h, j, 0)].astype(F32)
        total = total + r1[n, h, j, 0].astype(F32) + r1[n, h, j, 1].astype(F32)
        s[n, h, j] = total.astype(BF16)
        if j == 2:
            push(s.at[n, h, 2, lo], f2.at[n, h, 0], ssem, f2_sem.at[n, h], right)
            push(s.at[n, h, 2, hi], f2.at[n, h, 1], ssem, f2_sem.at[n, h], left)
        elif j == 1:
            push(s.at[n, h, 1, hi], r2.at[n, h, 0, hi], ssem, r2_sem.at[n, h], right)
        elif j == 3:
            push(s.at[n, h, 3, lo], r2.at[n, h, 1, lo], ssem, r2_sem.at[n, h], left)

    def task_f2(n, h):
        axis_b = ring(h)[1]
        right, left = grid_device(axis_b, 1), grid_device(axis_b, -1)
        ssem = send.at[n, h, 2]
        arrived(f2.at[n, h], f2_sem.at[n, h])
        f2[n, h, 0] = (f2[n, h, 0].astype(F32) + s[n, h, 1, lo].astype(F32)).astype(BF16)
        push(f2.at[n, h, 0], r2.at[n, h, 0, lo], ssem, r2_sem.at[n, h], right)
        f2[n, h, 1] = (f2[n, h, 1].astype(F32) + s[n, h, 3, hi].astype(F32)).astype(BF16)
        push(f2.at[n, h, 1], r2.at[n, h, 1, hi], ssem, r2_sem.at[n, h], left)

    def share(n, h, j, i, axis, delta):
        axis_a = ring(h)[0]
        nj, ni = (j, (i - delta) % SIDE) if axis == axis_a else ((j - delta) % SIDE, i)
        far = 2 in (ni if axis == axis_a else nj,)
        block = g.at[n, h, slot(h, j, i)]
        if far:
            block = block.at[lo if delta == 1 else hi]
        push(block, block, send.at[n, h, 3], g_sem.at[n, h, nj, ni], grid_device(axis, delta))

    def task_d2(n, h):
        axis_a, axis_b, _, _ = ring(h)
        arrived(r2.at[n, h], r2_sem.at[n, h])
        mine = slot(h, 0, 0)

        @pl.loop(0, 4)
        def _(at):
            rows = pl.ds(pl.multiple_of(at * 16, 16), 16)
            hidden = s[n, h, 0, rows].astype(F32) + r2[n, h, 0, rows].astype(F32) + r2[n, h, 1, rows].astype(F32)
            cdf, density = gelu_parts(hidden)
            act[rows, columns(n, h)] = (hidden * cdf).astype(BF16)
            grad = cot[rows, columns(n, h)].astype(F32) * (cdf + hidden * density)
            g[n, h, mine, rows] = grad.astype(BF16)

        for axis in (axis_b, axis_a):
            for delta in (1, -1):
                share(n, h, 0, 0, axis, delta)

    def block_here(n, h, j, i):
        arrived(g.at[n, h, slot(h, j, i)], g_sem.at[n, h, j, i])

    def task_b(n, h, j):
        axis_a = ring(h)[0]
        block_here(n, h, j, 3)
        share(n, h, j, 3, axis_a, 1)
        block_here(n, h, j, 1)
        share(n, h, j, 1, axis_a, -1)

    def task_a1(n, h):
        axis_a, axis_b, _, _ = ring(h)
        for j, delta in ((3, 1), (1, -1)):
            block_here(n, h, j, 0)
            share(n, h, j, 0, axis_b, delta)
            share(n, h, j, 0, axis_a, 1)
            share(n, h, j, 0, axis_a, -1)

    def task_a2(n, h):
        axis_a = ring(h)[0]
        block_here(n, h, 2, 0)
        share(n, h, 2, 0, axis_a, 1)
        share(n, h, 2, 0, axis_a, -1)

    finished = (set(), set())
    pushed = set()

    def task_c(n, h, j, last):
        block_here(n, h, j, 2)
        at = group(h, j)
        rows = g[n, h, pl.ds(SIDE * at, SIDE)].reshape(256, fh)
        delta_t = lax.dot_general(
            rows, w[:, columns(n, h)], (((1,), (1,)), ((), ())), preferred_element_type=F32
        )
        if h == 0:
            four = pl.ds(SIDE * at, SIDE)
            delta_t = delta_t.reshape(SIDE, 64, 384)
            gt[four] = gt[four] + delta_t
        else:
            for at_y in range(SIDE):
                piece = delta_t[64 * at_y : 64 * at_y + 64]
                gt[SIDE * at_y + at] = gt[SIDE * at_y + at] + piece
        if n == NCH - 1:
            finished[h].add(j)
            for jy in finished[0]:
                for ix in finished[1]:
                    if (jy, ix) not in pushed:
                        pushed.add((jy, ix))
                        send_tokens(jy, ix)
        delta_w = jnp.dot(tok_t[h, at], rows, preferred_element_type=F32)
        if j == 0:
            gw[h] = delta_w
        elif not last:
            gw[h] = gw[h] + delta_w
        else:
            gwb[n, h] = (gw[h] + delta_w).astype(BF16)
            cols = columns(n, h)
            push(gwb.at[n, h], other_hbm.at[:, cols], dep_send.at[n, h], dep_recv.at[n, h], other)
            pltpu.make_async_copy(gwb.at[n, h], own_hbm.at[:, cols], out_sem.at[n, h]).start()

    def send_tokens(jy, ix):
        at = ((yx[0] + jy) % SIDE) * SIDE + (yx[1] + ix) % SIDE
        zsend[at] = gt[at].astype(BF16)
        to = at // 2
        ahead = (to - row + ROWS) % ROWS

        @pl.when(ahead != 0)
        def _():
            place = ROWS - 1 - ahead
            push(zsend.at[at], zrecv.at[place, at % 2], zs_send.at[0], zs_recv.at[0], {"row": to})

    cot_waited = False
    done_transposes = False
    for name, n, j in schedule():
        if name == "D2" and not cot_waited:
            loads[2].wait()
            cot_waited = True
        if name == "I":
            for h in (0, 1):
                task_i(n, h, j)
            if not done_transposes and j == 0:
                transposes()
                done_transposes = True
        for h in (0, 1):
            if name == "F":
                task_f(n, h, j)
            elif name == "D":
                task_d(n, h, j)
            elif name == "F2":
                task_f2(n, h)
            elif name == "D2":
                task_d2(n, h)
            elif name == "B":
                task_b(n, h, j)
            elif name == "A1":
                task_a1(n, h)
            elif name == "A2":
                task_a2(n, h)
            elif name == "C":
                task_c(n, h, j, j == 2)

    act_out = pltpu.make_async_copy(act, act_hbm, local_sem.at[0])
    act_out.start()
    arrived(zrecv, zs_recv.at[0])
    for at in range(2):
        total = gt[2 * row + at].astype(BF16).astype(F32)
        for place in range(ROWS - 1):
            total = total + zrecv[place, at].astype(F32)
        zsend[2 * row + at] = total.astype(BF16)
    gt_out = pltpu.make_async_copy(zsend.at[pl.ds(2 * row, 2)], gt_hbm, local_sem.at[1])
    gt_out.start()

    for n in range(NCH):
        for h in (0, 1):
            sent(r1.at[n, h], send.at[n, h, 0])
            sent(s.at[n, h], send.at[n, h, 1])
            sent(s.at[n, h, pl.ds(0, 3)], send.at[n, h, 2])
            sent(g.at[n, h, pl.ds(0, 15)], send.at[n, h, 3])
            cols = columns(n, h)
            pltpu.make_async_copy(gwb.at[n, h], own_hbm.at[:, cols], out_sem.at[n, h]).wait()
            done = remote(gwb.at[n, h], other_hbm.at[:, cols], dep_send.at[n, h], dep_recv.at[n, h], other)
            done.wait_send()
            done.wait_recv()
    for k in range(8):
        ref = two(0) if k < 6 else tok.at[0, 0]
        sent(ref, z_send.at[k])
    sent(zsend.at[pl.ds(0, 14)], zs_send.at[0])
    act_out.wait()
    gt_out.wait()


def local(tokens, weight, cotangent):
    d, f = weight.shape
    fh = f // (2 * NCH)
    any_spec = pl.BlockSpec(memory_space=pl.ANY)
    vmem = pltpu.VMEM
    dma = pltpu.SemaphoreType.DMA
    act, own, other, gt = pl.pallas_call(
        kernel,
        out_shape=(
            jax.ShapeDtypeStruct(cotangent.shape, BF16),
            jax.ShapeDtypeStruct(weight.shape, BF16),
            jax.ShapeDtypeStruct(weight.shape, BF16),
            jax.ShapeDtypeStruct((2, 64, d), BF16),
        ),
        in_specs=[any_spec] * 3,
        out_specs=(any_spec,) * 4,
        scratch_shapes=[
            vmem(weight.shape, BF16),
            vmem(cotangent.shape, BF16),
            vmem(cotangent.shape, BF16),
            vmem((2, 16, 64, d), BF16),
            vmem((2, SIDE, d, 256), BF16),
            vmem((NCH, 2, 16, 64, fh), BF16),
            vmem((NCH, 2, SIDE, 2, 32, fh), BF16),
            vmem((NCH, 2, SIDE, 2, 64, fh), BF16),
            vmem((NCH, 2, SIDE, 64, fh), BF16),
            vmem((NCH, 2, 2, 32, fh), BF16),
            vmem((NCH, 2, 2, 64, fh), BF16),
            vmem((NCH, 2, 16, 64, fh), BF16),
            vmem((2, d, fh), F32),
            vmem((NCH, 2, d, fh), BF16),
            vmem((16, 64, d), F32),
            vmem((16, 64, d), BF16),
            vmem((ROWS - 1, 2, 64, d), BF16),
            dma((3,)),
            dma((NCH, 2)),
            dma((8,)),
            dma((8,)),
            dma((NCH, 2, 4)),
            dma((NCH, 2, SIDE)),
            dma((NCH, 2, SIDE)),
            dma((NCH, 2)),
            dma((NCH, 2)),
            dma((NCH, 2, SIDE, SIDE)),
            dma((NCH, 2)),
            dma((NCH, 2)),
            dma((1,)),
            dma((1,)),
        ],
        compiler_params=pltpu.CompilerParams(
            collective_id=0, has_side_effects=True, vmem_limit_bytes=56 * 2**20
        ),
    )(tokens.reshape(2, 64, d), weight, cotangent)
    grad_weight = (own.astype(F32) + other.astype(F32)).astype(BF16)
    return (act, gt.reshape(128, d), grad_weight)


def solution(mesh):
    placed = (P(("depth", "row"), "col"), P("col", "row"), P(("depth", "col"), "row"))
    return jax.shard_map(
        local,
        mesh=mesh,
        in_specs=placed,
        out_specs=(P(("depth", "col"), "row"), P(("depth", "row"), "col"), P("col", "row")),
        check_vma=False,
    )
```

```python
import functools
import math

import jax
import jax.numpy as jnp
from jax import lax
from jax.experimental import pallas as pl
from jax.experimental.pallas import tpu as pltpu
from jax.sharding import PartitionSpec as P

MESH = pl.DeviceIdType.MESH
NCH = 2
SIDE = 4
ROWS = 8
BF16 = jnp.bfloat16
F32 = jnp.float32


def gelu_parts(hidden):
    cdf = 0.5 * (1.0 + lax.erf(hidden * (1.0 / math.sqrt(2.0))))
    density = jnp.exp(-0.5 * hidden * hidden) * (1.0 / math.sqrt(2.0 * math.pi))
    return (cdf, density)


GATHERS = ((0, 0, 64, False), (1, 0, 32, False), (1, 32, 32, False))


def schedule():
    t = [("Z", 0, 1), ("IW", 0, 0), ("Z", 0, 2), ("IW", 0, 1), ("FP", 0, 0), ("FQ", 0, 0)]
    t += [("Z", 0, 3), ("IW", 0, 2), ("FP", 0, 1), ("FQ", 0, 1), ("DP", 0, 0)]
    t += [("Z", 0, 4), ("IW", 0, 3), ("FP", 0, 2), ("FQ", 0, 2), ("DP", 0, 1), ("tokens", 0, 0)]
    t += [("I", 1, 2), ("FP", 0, 3), ("FQ", 0, 3), ("I", 1, 1), ("DP", 0, 2), ("DQ", 0, 2)]
    t += [("I", 1, 3), ("DQ", 0, 1), ("DP", 0, 3), ("I", 1, 0), ("DQ", 0, 3), ("DQ", 0, 0)]
    t += [("F2", 0, 0), ("D2", 0, 0), ("S", 0, 0), ("transposes", 0, 0)]
    t += [("F", 1, 2), ("F", 1, 1), ("A1", 0, 0), ("D", 1, 2), ("F", 1, 3), ("D", 1, 1)]
    t += [("B", 0, 0), ("F", 1, 0), ("A2", 0, 0), ("D", 1, 3), ("D", 1, 0)]
    t += [("B", 0, 1), ("B", 0, 3), ("F2", 1, 0), ("T", 0, 0), ("B", 0, 2)]
    t += [("D2", 1, 0), ("S", 1, 0), ("S", 2, 0)]
    t += [("T", 0, 1), ("A1", 1, 0), ("T", 0, 3), ("A1", 2, 0), ("B", 1, 0), ("T", 0, 2), ("W", 0, 0)]
    t += [("A2", 1, 0), ("B", 2, 0), ("A2", 2, 0), ("B", 1, 1), ("B", 1, 3), ("B", 2, 1), ("B", 2, 3)]
    t += [("T", 1, 0), ("B", 1, 2), ("T", 2, 0), ("B", 2, 2), ("T", 1, 1), ("T", 1, 3), ("T", 1, 2)]
    t += [("W", 1, 0), ("T", 2, 1), ("T", 2, 3), ("T", 2, 2), ("W", 2, 0)]
    return t


def kernel(
    tok_hbm, w_hbm, cot_hbm, act_hbm, own_hbm, other_hbm, gt_hbm,
    w, cot, act, tok, tok_t, part, f1, r1, s, f2, r2, g, gw, gwb, gt, zsend, zrecv,
    local_sem, out_sem, z_send, z_recv, send, g_send, f1_sem, r1_sem, f2_sem, r2_sem, g_sem,
    dep_send, dep_recv, zs_send, zs_recv,
):
    fh = part.shape[-1]
    half = 32
    depth, row, col = (lax.axis_index(a) for a in ("depth", "row", "col"))
    yx = (col // SIDE, col % SIDE)
    lo, hi = pl.ds(0, half), pl.ds(half, half)

    loads = [
        pltpu.make_async_copy(tok_hbm, tok.at[0, pl.ds(2 * row, 2)], local_sem.at[0]),
        pltpu.make_async_copy(w_hbm, w, local_sem.at[1]),
        pltpu.make_async_copy(cot_hbm, cot, local_sem.at[2]),
    ]
    for load in loads:
        load.start()

    def grid_device(axis, delta):
        at = list(yx)
        at[axis] = (at[axis] + delta + SIDE) % SIDE
        return {"col": at[0] * SIDE + at[1]}

    def row_device(delta):
        return {"row": (row + delta + ROWS) % ROWS}

    other = {"depth": 1 - depth}

    barrier = pltpu.get_barrier_semaphore()
    peers = [row_device(d) for d in range(1, ROWS)]
    peers += [grid_device(axis, delta) for axis in (0, 1) for delta in (1, 2, 3)]
    peers += [other]
    for peer in peers:
        pl.semaphore_signal(barrier, inc=1, device_id=peer, device_id_type=MESH)
    loads[0].wait()
    pl.semaphore_wait(barrier, len(peers))

    def remote(src, dst, ssem, rsem, device):
        return pltpu.make_async_remote_copy(
            src_ref=src, dst_ref=dst, send_sem=ssem, recv_sem=rsem,
            device_id=device, device_id_type=MESH,
        )

    def push(src, dst, ssem, rsem, device):
        remote(src, dst, ssem, rsem, device).start()

    def arrived(ref, rsem):
        remote(ref, ref, send.at[0, 0, 0], rsem, other).wait_recv()

    def sent(ref, ssem):
        remote(ref, ref, ssem, f2_sem.at[0, 0], other).wait_send()

    def piece(delta, k):
        return tok.at[0, 2 * ((row + delta + ROWS) % ROWS) + k]

    def hand_on(delta, k, way):
        sem = 4 * abs(delta) + 2 * k + way
        push(piece(delta, k), piece(delta, k), z_send.at[sem], z_recv.at[sem], row_device(1 - 2 * way))

    for k in (0, 1):
        hand_on(0, k, 0)
        hand_on(0, k, 1)
    gt[...] = jnp.zeros_like(gt)

    def task_z(step):
        for k in (0, 1):
            for way in (0, 1):
                if step == 4 and k != way:
                    continue
                delta = -step if way == 0 else step
                arrived(piece(delta, k), z_recv.at[4 * (step - 1) + 2 * k + way])
                if step < 3 or (step == 3 and k == way):
                    hand_on(delta, k, way)

    def task_tokens():
        for at_y in range(SIDE):
            for at_x in range(SIDE):
                tok[1, at_x * SIDE + at_y] = tok[0, at_y * SIDE + at_x]

    def task_transposes():
        for h in range(2):
            for t in range(2):
                tok_t[h, t] = tok[h, :, pl.ds(32 * t, 32)].reshape(512, 384).T

    def ring(h):
        axis_a, axis_b = (1, 0) if h == 0 else (0, 1)
        return axis_a, axis_b, yx[axis_a], yx[axis_b]

    def slot(h, j, i):
        _, _, a, b = ring(h)
        return ((b + j) % SIDE) * SIDE + (a + i) % SIDE

    def columns(n, h):
        return pl.ds((2 * n + h) * fh, fh)

    def group(h, j):
        _, _, _, b = ring(h)
        return (b + j) % SIDE

    toward = 1 - 2 * (row % 2)
    waves = [row // 2, (row // 2 - toward + SIDE) % SIDE, (row // 2 + toward + SIDE) % SIDE, (row // 2 + 2) % SIDE]

    def first_sends(n, h, j):
        axis_a = ring(h)[0]
        right, left = grid_device(axis_a, 1), grid_device(axis_a, -1)
        ssem = send.at[n, h, 0]
        far = part.at[n, h, slot(h, j, 2)]
        push(far.at[lo], f1.at[n, h, j, 0], ssem, f1_sem.at[n, h, j, 0], right)
        push(far.at[hi], f1.at[n, h, j, 1], ssem, f1_sem.at[n, h, j, 1], left)
        push(part.at[n, h, slot(h, j, 1), hi], r1.at[n, h, j, 0, hi], ssem, r1_sem.at[n, h, j], right)
        push(part.at[n, h, slot(h, j, 3), lo], r1.at[n, h, j, 1, lo], ssem, r1_sem.at[n, h, j], left)

    def task_iw(n, wave):
        at_y = waves[wave]
        if wave == 0:
            loads[1].wait()
        four = pl.ds(SIDE * at_y, SIDE)
        x = tok[0, four].reshape(256, 384)
        y = jnp.dot(x, w[:, columns(n, 0)], preferred_element_type=F32).astype(BF16)
        part[n, 0, four] = y.reshape(SIDE, 64, fh)
        first_sends(n, 0, (at_y - yx[0] + SIDE) % SIDE)
        y = jnp.dot(x, w[:, columns(n, 1)], preferred_element_type=F32).astype(BF16)
        for at_x in range(SIDE):
            part[n, 1, SIDE * at_x + at_y] = y[64 * at_x : 64 * at_x + 64]
        role = (at_y - yx[0] + SIDE) % SIDE
        right, left = grid_device(0, 1), grid_device(0, -1)
        ssem = send.at[n, 1, 0]

        @pl.when(role == 2)
        def _():
            for j in range(SIDE):
                far = part.at[n, 1, slot(1, j, 2)]
                push(far.at[lo], f1.at[n, 1, j, 0], ssem, f1_sem.at[n, 1, j, 0], right)
                push(far.at[hi], f1.at[n, 1, j, 1], ssem, f1_sem.at[n, 1, j, 1], left)

        @pl.when(role == 1)
        def _():
            for j in range(SIDE):
                push(part.at[n, 1, slot(1, j, 1), hi], r1.at[n, 1, j, 0, hi], ssem, r1_sem.at[n, 1, j], right)

        @pl.when(role == 3)
        def _():
            for j in range(SIDE):
                push(part.at[n, 1, slot(1, j, 3), lo], r1.at[n, 1, j, 1, lo], ssem, r1_sem.at[n, 1, j], left)

    def task_i(n, h, j):
        four = pl.ds(SIDE * group(h, j), SIDE)
        x = tok[h, four].reshape(256, 384)
        y = jnp.dot(x, w[:, columns(n, h)], preferred_element_type=F32).astype(BF16)
        part[n, h, four] = y.reshape(SIDE, 64, fh)
        first_sends(n, h, j)

    def forward(n, h, j, way):
        axis_a = ring(h)[0]
        device = grid_device(axis_a, 1 - 2 * way)
        rows, near = (lo, 1) if way == 0 else (hi, 3)
        arrived(f1.at[n, h, j, way], f1_sem.at[n, h, j, way])
        f1[n, h, j, way] = (
            f1[n, h, j, way].astype(F32) + part[n, h, slot(h, j, near), rows].astype(F32)
        ).astype(BF16)
        push(f1.at[n, h, j, way], r1.at[n, h, j, way, rows], send.at[n, h, 1], r1_sem.at[n, h, j], device)

    def task_f(n, h, j):
        forward(n, h, j, 0)
        forward(n, h, j, 1)

    def task_fq(n, wave):
        role = (waves[wave] - yx[0] + SIDE) % SIDE

        @pl.when(role == 1)
        def _():
            for j in range(SIDE):
                forward(n, 1, j, 0)

        @pl.when(role == 3)
        def _():
            for j in range(SIDE):
                forward(n, 1, j, 1)

    def sum_first(n, h, j):
        arrived(r1.at[n, h, j], r1_sem.at[n, h, j])
        total = part[n, h, slot(h, j, 0)].astype(F32)
        total = total + r1[n, h, j, 0].astype(F32) + r1[n, h, j, 1].astype(F32)
        s[n, h, j] = total.astype(BF16)

    def second_sends(n, h, j):
        axis_b = ring(h)[1]
        right, left = grid_device(axis_b, 1), grid_device(axis_b, -1)
        ssem = send.at[n, h, 2]
        if j == 2:
            push(s.at[n, h, 2, lo], f2.at[n, h, 0], ssem, f2_sem.at[n, h], right)
            push(s.at[n, h, 2, hi], f2.at[n, h, 1], ssem, f2_sem.at[n, h], left)
        elif j == 1:
            push(s.at[n, h, 1, hi], r2.at[n, h, 0, hi], ssem, r2_sem.at[n, h], right)
        elif j == 3:
            push(s.at[n, h, 3, lo], r2.at[n, h, 1, lo], ssem, r2_sem.at[n, h], left)

    def task_d(n, h, j):
        sum_first(n, h, j)
        second_sends(n, h, j)

    def task_dp(n, wave):
        j = (waves[wave] - yx[0] + SIDE) % SIDE
        sum_first(n, 0, j)
        for role in (1, 2, 3):
            pl.when(j == role)(functools.partial(second_sends, n, 0, role))

    def task_f2(n, h):
        axis_b = ring(h)[1]
        right, left = grid_device(axis_b, 1), grid_device(axis_b, -1)
        ssem = send.at[n, h, 2]
        arrived(f2.at[n, h], f2_sem.at[n, h])
        f2[n, h, 0] = (f2[n, h, 0].astype(F32) + s[n, h, 1, lo].astype(F32)).astype(BF16)
        push(f2.at[n, h, 0], r2.at[n, h, 0, lo], ssem, r2_sem.at[n, h], right)
        f2[n, h, 1] = (f2[n, h, 1].astype(F32) + s[n, h, 3, hi].astype(F32)).astype(BF16)
        push(f2.at[n, h, 1], r2.at[n, h, 1, hi], ssem, r2_sem.at[n, h], left)

    def task_d2(n, h):
        arrived(r2.at[n, h], r2_sem.at[n, h])
        mine = slot(h, 0, 0)

        @pl.loop(0, 4)
        def _(at):
            rows = pl.ds(pl.multiple_of(at * 16, 16), 16)
            hidden = s[n, h, 0, rows].astype(F32) + r2[n, h, 0, rows].astype(F32) + r2[n, h, 1, rows].astype(F32)
            cdf, density = gelu_parts(hidden)
            act[rows, columns(n, h)] = (hidden * cdf).astype(BF16)
            grad = cot[rows, columns(n, h)].astype(F32) * (cdf + hidden * density)
            g[n, h, mine, rows] = grad.astype(BF16)

    def block(c, h, j, i):
        n, start, size, _ = GATHERS[c]
        return g.at[n, h, slot(h, j, i), pl.ds(start, size)]

    def share(c, h, j, i, axis, delta):
        n, start, size, straight = GATHERS[c]
        axis_a = ring(h)[0]
        nj, ni = (j, (i - delta) % SIDE) if axis == axis_a else ((j - delta) % SIDE, i)
        ref = block(c, h, j, i)
        if delta != 2 and 2 in (ni if axis == axis_a else nj,):
            ref = g.at[n, h, slot(h, j, i), pl.ds(start if delta == 1 else start + size // 2, size // 2)]
        push(ref, ref, g_send.at[c, h], g_sem.at[c, h, nj, ni], grid_device(axis, delta))

    def ways(c):
        return (1, -1, 2) if GATHERS[c][3] else (1, -1)

    here = set()

    def block_here(c, h, j, i):
        if (c, h, j, i) not in here:
            here.add((c, h, j, i))
            arrived(block(c, h, j, i), g_sem.at[c, h, j, i])

    def task_s(c, h):
        axis_a, axis_b, _, _ = ring(h)
        here.add((c, h, 0, 0))
        for axis in (axis_b, axis_a):
            for delta in ways(c):
                share(c, h, 0, 0, axis, delta)

    def task_a1(c, h):
        axis_a, axis_b, _, _ = ring(h)
        for j, delta in ((3, 1), (1, -1)):
            block_here(c, h, j, 0)
            if not GATHERS[c][3]:
                share(c, h, j, 0, axis_b, delta)
        for j in (3, 1):
            for delta in ways(c):
                share(c, h, j, 0, axis_a, delta)

    def task_a2(c, h):
        axis_a = ring(h)[0]
        block_here(c, h, 2, 0)
        for delta in ways(c):
            share(c, h, 2, 0, axis_a, delta)

    def task_b(c, h, j):
        axis_a = ring(h)[0]
        if not GATHERS[c][3]:
            block_here(c, h, j, 3)
            share(c, h, j, 3, axis_a, 1)
            block_here(c, h, j, 1)
            share(c, h, j, 1, axis_a, -1)

    finished = set()

    def task_t(c, h, i):
        n, start, size, _ = GATHERS[c]
        rows = pl.ds(start, size)
        at_x = (yx[1] + i) % SIDE
        for k in range(SIDE):
            block_here(c, h, *((k, i) if h == 0 else (i, k)))
        if h == 0:
            blocks = jnp.concatenate([g[n, h, SIDE * at_y + at_x, rows] for at_y in range(SIDE)], axis=0)
        else:
            blocks = g[n, h, pl.ds(SIDE * at_x, SIDE), rows].reshape(SIDE * size, fh)
        terms = lax.dot_general(
            blocks, w[:, columns(n, h)], (((1,), (1,)), ((), ())), preferred_element_type=F32
        )
        for at_y in range(SIDE):
            at = SIDE * at_y + at_x
            gt[at, rows] = gt[at, rows] + terms[size * at_y : size * at_y + size]
        finished.add((c, h, i))
        if n == NCH - 1 and (c, 1 - h, i) in finished:
            for at_y in range(SIDE):
                send_tokens(SIDE * at_y + at_x, rows)

    def send_tokens(at, rows):
        zsend[at, rows] = gt[at, rows].astype(BF16)
        to = at // 2
        ahead = (to - row + ROWS) % ROWS

        @pl.when(ahead != 0)
        def _():
            place = ROWS - 1 - ahead
            push(zsend.at[at, rows], zrecv.at[place, at % 2, rows], zs_send.at[0], zs_recv.at[0], {"row": to})

    def task_w(c, h):
        n, start, size, _ = GATHERS[c]
        for j in range(SIDE):
            for i in range(SIDE):
                block_here(c, h, j, i)
        total = None
        for t in range(start // half, (start + size) // half):
            rows = g[n, h, :, pl.ds(half * t, half)].reshape(512, fh)
            term = jnp.dot(tok_t[h, t], rows, preferred_element_type=F32)
            total = term if total is None else total + term
        if start > 0:
            total = gw[h] + total
        if start + size < 64:
            gw[h] = total
        else:
            gwb[n, h] = total.astype(BF16)
            cols = columns(n, h)
            push(gwb.at[n, h], other_hbm.at[:, cols], dep_send.at[n, h], dep_recv.at[n, h], other)
            pltpu.make_async_copy(gwb.at[n, h], own_hbm.at[:, cols], out_sem.at[n, h]).start()

    both = {"F": task_f, "D": task_d, "I": task_i, "B": task_b, "T": task_t}
    both_once = {"F2": task_f2, "D2": task_d2, "S": task_s, "A1": task_a1, "A2": task_a2, "W": task_w}
    cot_waited = False
    for name, n, j in schedule():
        if name == "D2" and not cot_waited:
            loads[2].wait()
            cot_waited = True
        if name in both:
            for h in (0, 1):
                both[name](n, h, j)
        elif name in both_once:
            for h in (0, 1):
                both_once[name](n, h)
        elif name == "Z":
            task_z(j)
        elif name == "IW":
            task_iw(n, j)
        elif name == "FP":
            task_f(n, 0, (waves[j] - yx[0] + SIDE) % SIDE)
        elif name == "FQ":
            task_fq(n, j)
        elif name == "DP":
            task_dp(n, j)
        elif name == "DQ":
            task_d(n, 1, j)
        elif name == "tokens":
            task_tokens()
        elif name == "transposes":
            task_transposes()

    act_out = pltpu.make_async_copy(act, act_hbm, local_sem.at[0])
    act_out.start()
    arrived(zrecv, zs_recv.at[0])
    for at in range(2):
        total = gt[2 * row + at].astype(BF16).astype(F32)
        for place in range(ROWS - 1):
            total = total + zrecv[place, at].astype(F32)
        zsend[2 * row + at] = total.astype(BF16)
    gt_out = pltpu.make_async_copy(zsend.at[pl.ds(2 * row, 2)], gt_hbm, local_sem.at[1])
    gt_out.start()

    for n in range(NCH):
        for h in (0, 1):
            sent(r1.at[n, h], send.at[n, h, 0])
            sent(s.at[n, h], send.at[n, h, 1])
            sent(s.at[n, h, pl.ds(0, 3)], send.at[n, h, 2])
            cols = columns(n, h)
            pltpu.make_async_copy(gwb.at[n, h], own_hbm.at[:, cols], out_sem.at[n, h]).wait()
            done = remote(gwb.at[n, h], other_hbm.at[:, cols], dep_send.at[n, h], dep_recv.at[n, h], other)
            done.wait_send()
            done.wait_recv()
    for c, (n, start, size, _) in enumerate(GATHERS):
        for h in (0, 1):
            sent(g.at[n, h, pl.ds(0, 15), pl.ds(start, size)], g_send.at[c, h])
    for delta in range(4):
        for k in (0, 1):
            for way in (0, 1):
                if delta < 3 or k == way:
                    sent(tok.at[0, 0], z_send.at[4 * delta + 2 * k + way])
    sent(zsend.at[pl.ds(0, 14)], zs_send.at[0])
    act_out.wait()
    gt_out.wait()


def local(tokens, weight, cotangent):
    d, f = weight.shape
    fh = f // (2 * NCH)
    any_spec = pl.BlockSpec(memory_space=pl.ANY)
    vmem = pltpu.VMEM
    dma = pltpu.SemaphoreType.DMA
    act, own, other, gt = pl.pallas_call(
        kernel,
        out_shape=(
            jax.ShapeDtypeStruct(cotangent.shape, BF16),
            jax.ShapeDtypeStruct(weight.shape, BF16),
            jax.ShapeDtypeStruct(weight.shape, BF16),
            jax.ShapeDtypeStruct((2, 64, d), BF16),
        ),
        in_specs=[any_spec] * 3,
        out_specs=(any_spec,) * 4,
        scratch_shapes=[
            vmem(weight.shape, BF16),
            vmem(cotangent.shape, BF16),
            vmem(cotangent.shape, BF16),
            vmem((2, 16, 64, d), BF16),
            vmem((2, 2, d, 512), BF16),
            vmem((NCH, 2, 16, 64, fh), BF16),
            vmem((NCH, 2, SIDE, 2, 32, fh), BF16),
            vmem((NCH, 2, SIDE, 2, 64, fh), BF16),
            vmem((NCH, 2, SIDE, 64, fh), BF16),
            vmem((NCH, 2, 2, 32, fh), BF16),
            vmem((NCH, 2, 2, 64, fh), BF16),
            vmem((NCH, 2, 16, 64, fh), BF16),
            vmem((2, d, fh), F32),
            vmem((NCH, 2, d, fh), BF16),
            vmem((16, 64, d), F32),
            vmem((16, 64, d), BF16),
            vmem((ROWS - 1, 2, 64, d), BF16),
            dma((3,)),
            dma((NCH, 2)),
            dma((16,)),
            dma((16,)),
            dma((NCH, 2, 3)),
            dma((len(GATHERS), 2)),
            dma((NCH, 2, SIDE, 2)),
            dma((NCH, 2, SIDE)),
            dma((NCH, 2)),
            dma((NCH, 2)),
            dma((len(GATHERS), 2, SIDE, SIDE)),
            dma((NCH, 2)),
            dma((NCH, 2)),
            dma((1,)),
            dma((1,)),
        ],
        compiler_params=pltpu.CompilerParams(
            collective_id=0, has_side_effects=True, vmem_limit_bytes=48 * 2**20
        ),
    )(tokens.reshape(2, 64, d), weight, cotangent)
    grad_weight = (own.astype(F32) + other.astype(F32)).astype(BF16)
    return (act, gt.reshape(128, d), grad_weight)


def solution(mesh):
    placed = (P(("depth", "row"), "col"), P("col", "row"), P(("depth", "col"), "row"))
    return jax.shard_map(
        local,
        mesh=mesh,
        in_specs=placed,
        out_specs=(P(("depth", "col"), "row"), P(("depth", "row"), "col"), P("col", "row")),
        check_vma=False,
    )
```

```python
import functools
import math

import jax
import jax.numpy as jnp
from jax import lax
from jax.experimental import pallas as pl
from jax.experimental.pallas import tpu as pltpu
from jax.sharding import PartitionSpec as P

MESH = pl.DeviceIdType.MESH
NCH = 2
X_FIRST = (3, 2)
SIDE = 4
ROWS = 8
BF16 = jnp.bfloat16
F32 = jnp.float32


def gelu_parts(hidden):
    cdf = 0.5 * (1.0 + lax.erf(hidden * (1.0 / math.sqrt(2.0))))
    density = jnp.exp(-0.5 * hidden * hidden) * (1.0 / math.sqrt(2.0 * math.pi))
    return (cdf, density)


GATHERS = ((0, 0, 64, False), (1, 0, 64, False))


ORDER = (
    ("Z", 0, 1), ("IW", 0, 0), ("FP", 0, 0), ("Z", 0, 2), ("IW", 0, 1), ("DP", 0, 0), ("FP", 0, 1),
    ("Z", 0, 3), ("Z", 0, 4), ("IW", 0, 2), ("IW", 0, 3), ("tokens", 0, 0), ("I1", 0, 0), ("I1", 0, 1),
    ("I1", 0, 2), ("I1", 0, 3), ("DP", 0, 1), ("I0", 1, 0), ("I0", 1, 1), ("I0", 1, 2), ("I0", 1, 3),
    ("FP", 0, 2), ("F1", 0, 0), ("I1", 1, 0), ("I1", 1, 1), ("F1", 0, 1), ("I1", 1, 2), ("I1", 1, 3),
    ("F1", 0, 2), ("transposes", 0, 0), ("FP", 0, 3), ("F1", 0, 3), ("D1", 0, 0), ("F0", 1, 0), ("F1", 1, 0),
    ("F0", 1, 1), ("F1", 1, 1), ("F0", 1, 2), ("D1", 0, 1), ("F1", 1, 2), ("F0", 1, 3), ("F1", 1, 3),
    ("DP", 0, 2), ("D1", 0, 2), ("D1", 0, 3), ("DP", 0, 3), ("D1", 1, 0), ("D0", 1, 0), ("D1", 1, 1),
    ("D0", 1, 1), ("D1", 1, 2), ("D0", 1, 2), ("D1", 1, 3), ("D0", 1, 3), ("G0", 0, 0), ("G1", 0, 0),
    ("G0", 1, 0), ("G1", 1, 0), ("H1", 0, 0), ("H0", 0, 0), ("S0", 0, 0), ("S1", 0, 0), ("H0", 1, 0),
    ("H1", 1, 0), ("S0", 1, 0), ("S1", 1, 0), ("A0", 0, 1), ("B0", 0, 0), ("B1", 0, 0), ("A1", 0, 1),
    ("A0", 1, 1), ("B0", 1, 0), ("B1", 1, 0), ("A1", 1, 1), ("A0", 0, 2), ("T0", 0, 0), ("T1", 0, 0),
    ("B0", 0, 3), ("B1", 0, 3), ("B0", 0, 1), ("B1", 0, 1), ("A1", 0, 2), ("A0", 1, 2), ("T0", 1, 0),
    ("T1", 1, 0), ("B0", 1, 3), ("B1", 1, 3), ("B0", 1, 1), ("B1", 1, 1), ("A1", 1, 2), ("T1", 0, 3),
    ("T1", 0, 1), ("B0", 0, 2), ("T0", 0, 1), ("T0", 0, 3), ("B1", 0, 2), ("T1", 1, 3), ("T1", 1, 1),
    ("B0", 1, 2), ("T0", 1, 1), ("T0", 1, 3), ("B1", 1, 2), ("T1", 0, 2), ("T0", 0, 2), ("W0", 0, 0),
    ("T0", 1, 2), ("T1", 1, 2), ("W1", 0, 0), ("W0", 1, 0), ("W1", 1, 0),
)


def kernel(
    tok_hbm, w_hbm, cot_hbm, act_hbm, own_hbm, other_hbm, gt_hbm,
    w, cot, act, tok, tok_t, part, f1, r1, s, f2, r2, g, gw, gwb, gt, zsend, zrecv,
    local_sem, out_sem, z_send, z_recv, send, g_send, f1_sem, r1_sem, f2_sem, r2_sem, g_sem,
    dep_send, dep_recv, zs_send, zs_recv,
):
    fh = g.shape[-1]
    half = 32
    depth, row, col = (lax.axis_index(a) for a in ("depth", "row", "col"))
    yx = (col // SIDE, col % SIDE)
    lo, hi = pl.ds(0, half), pl.ds(half, half)

    loads = [
        pltpu.make_async_copy(tok_hbm, tok.at[0, pl.ds(2 * row, 2)], local_sem.at[0]),
        pltpu.make_async_copy(w_hbm, w, local_sem.at[1]),
        pltpu.make_async_copy(cot_hbm, cot, local_sem.at[2]),
    ]
    for load in loads:
        load.start()

    def grid_device(axis, delta):
        at = list(yx)
        at[axis] = (at[axis] + delta + SIDE) % SIDE
        return {"col": at[0] * SIDE + at[1]}

    def row_device(delta):
        return {"row": (row + delta + ROWS) % ROWS}

    other = {"depth": 1 - depth}

    barrier = pltpu.get_barrier_semaphore()
    peers = [row_device(d) for d in range(1, ROWS)]
    peers += [grid_device(axis, delta) for axis in (0, 1) for delta in (1, 2, 3)]
    peers += [other]
    for peer in peers:
        pl.semaphore_signal(barrier, inc=1, device_id=peer, device_id_type=MESH)
    loads[0].wait()
    pl.semaphore_wait(barrier, len(peers))

    def remote(src, dst, ssem, rsem, device):
        return pltpu.make_async_remote_copy(
            src_ref=src, dst_ref=dst, send_sem=ssem, recv_sem=rsem,
            device_id=device, device_id_type=MESH,
        )

    def push(src, dst, ssem, rsem, device):
        remote(src, dst, ssem, rsem, device).start()

    def arrived(ref, rsem):
        remote(ref, ref, send.at[0, 0, 0], rsem, other).wait_recv()

    def sent(ref, ssem):
        remote(ref, ref, ssem, f2_sem.at[0, 0], other).wait_send()

    def piece(delta, k):
        return tok.at[0, 2 * ((row + delta + ROWS) % ROWS) + k]

    def hand_on(delta, k, way, far=1):
        sem = 4 * (abs(delta) + far - 1) + 2 * k + way
        device = row_device(far * (1 - 2 * way))
        push(piece(delta, k), piece(delta, k), z_send.at[sem], z_recv.at[sem], device)

    for k in (0, 1):
        hand_on(0, k, 0)
        hand_on(0, k, 1)
    gt[...] = jnp.zeros_like(gt)

    def task_z(step):
        for k in (0, 1):
            for way in (0, 1):
                if step == 4 and k != way:
                    continue
                delta = -step if way == 0 else step
                arrived(piece(delta, k), z_recv.at[4 * (step - 1) + 2 * k + way])
                if step < 3:
                    hand_on(delta, k, way)
                if step == 2 and k == way:
                    hand_on(delta, k, way, 2)

    def task_tokens():
        for at_y in range(SIDE):
            for at_x in range(SIDE):
                tok[1, at_x * SIDE + at_y] = tok[0, at_y * SIDE + at_x]

    def task_transposes():
        for h in range(2):
            for t in range(2):
                tok_t[h, t] = tok[h, :, pl.ds(32 * t, 32)].reshape(512, 384).T

    def ring(h):
        axis_a, axis_b = (1, 0) if h == 0 else (0, 1)
        return axis_a, axis_b, yx[axis_a], yx[axis_b]

    def slot(h, j, i):
        _, _, a, b = ring(h)
        return ((b + j) % SIDE) * SIDE + (a + i) % SIDE

    def columns(n, h):
        return pl.ds((2 * n + h) * fh, fh)

    def summed(n, h):
        width = part[n][h].shape[-1]
        return pl.ds(2 * n * fh + (0 if h == 0 else 2 * fh - width), width)

    def group(h, j):
        _, _, _, b = ring(h)
        return (b + j) % SIDE

    toward = 1 - 2 * (row % 2)
    waves = [row // 2, (row // 2 - toward + SIDE) % SIDE, (row // 2 + toward + SIDE) % SIDE, (row // 2 + 2) % SIDE]

    def first_sends(n, h, j):
        axis_a = ring(h)[0]
        right, left = grid_device(axis_a, 1), grid_device(axis_a, -1)
        ssem = send.at[n, h, 0]
        far = part[n][h].at[slot(h, j, 2)]
        push(far.at[lo], f1[n][h].at[j, 0], ssem, f1_sem.at[n, h, j, 0], right)
        push(far.at[hi], f1[n][h].at[j, 1], ssem, f1_sem.at[n, h, j, 1], left)
        push(part[n][h].at[slot(h, j, 1), hi], r1[n][h].at[j, 0, hi], ssem, r1_sem.at[n, h, j], right)
        push(part[n][h].at[slot(h, j, 3), lo], r1[n][h].at[j, 1, lo], ssem, r1_sem.at[n, h, j], left)

    def task_iw(n, wave):
        if wave == 0:
            loads[1].wait()
        task_i(n, 0, (waves[wave] - yx[0] + SIDE) % SIDE)

    def task_i(n, h, j):
        four = pl.ds(SIDE * group(h, j), SIDE)
        x = tok[h, four].reshape(256, 384)
        y = jnp.dot(x, w[:, summed(n, h)], preferred_element_type=F32).astype(BF16)
        part[n][h][four] = y.reshape(SIDE, 64, y.shape[-1])
        first_sends(n, h, j)

    def forward(n, h, j, way):
        axis_a = ring(h)[0]
        device = grid_device(axis_a, 1 - 2 * way)
        rows, near = (lo, 1) if way == 0 else (hi, 3)
        arrived(f1[n][h].at[j, way], f1_sem.at[n, h, j, way])
        f1[n][h][j, way] = (
            f1[n][h][j, way].astype(F32) + part[n][h][slot(h, j, near), rows].astype(F32)
        ).astype(BF16)
        push(f1[n][h].at[j, way], r1[n][h].at[j, way, rows], send.at[n, h, 1], r1_sem.at[n, h, j], device)

    def task_f(n, h, j):
        forward(n, h, j, 0)
        forward(n, h, j, 1)

    def sum_first(n, h, j):
        arrived(r1[n][h].at[j], r1_sem.at[n, h, j])
        total = part[n][h][slot(h, j, 0)].astype(F32)
        total = total + r1[n][h][j, 0].astype(F32) + r1[n][h][j, 1].astype(F32)
        s[n][h][j] = total.astype(BF16)

    def second_sends(n, h, j):
        axis_b = ring(h)[1]
        right, left = grid_device(axis_b, 1), grid_device(axis_b, -1)
        ssem = send.at[n, h, 2]
        if j == 2:
            push(s[n][h].at[2, lo], f2[n][h].at[0], ssem, f2_sem.at[n, h], right)
            push(s[n][h].at[2, hi], f2[n][h].at[1], ssem, f2_sem.at[n, h], left)
        elif j == 1:
            push(s[n][h].at[1, hi], r2[n][h].at[0, hi], ssem, r2_sem.at[n, h], right)
        elif j == 3:
            push(s[n][h].at[3, lo], r2[n][h].at[1, lo], ssem, r2_sem.at[n, h], left)

    def task_d(n, h, j):
        sum_first(n, h, j)
        second_sends(n, h, j)

    def task_dp(n, wave):
        j = (waves[wave] - yx[0] + SIDE) % SIDE
        sum_first(n, 0, j)
        for role in (1, 2, 3):
            pl.when(j == role)(functools.partial(second_sends, n, 0, role))

    def task_f2(n, h):
        axis_b = ring(h)[1]
        right, left = grid_device(axis_b, 1), grid_device(axis_b, -1)
        ssem = send.at[n, h, 2]
        arrived(f2[n][h], f2_sem.at[n, h])
        f2[n][h][0] = (f2[n][h][0].astype(F32) + s[n][h][1, lo].astype(F32)).astype(BF16)
        push(f2[n][h].at[0], r2[n][h].at[0, lo], ssem, r2_sem.at[n, h], right)
        f2[n][h][1] = (f2[n][h][1].astype(F32) + s[n][h][3, hi].astype(F32)).astype(BF16)
        push(f2[n][h].at[1], r2[n][h].at[1, hi], ssem, r2_sem.at[n, h], left)

    def task_d2(n, h):
        arrived(r2[n][h], r2_sem.at[n, h])

        @pl.loop(0, 4)
        def _(at):
            rows = pl.ds(pl.multiple_of(at * 16, 16), 16)
            hidden = s[n][h][0, rows].astype(F32) + r2[n][h][0, rows].astype(F32) + r2[n][h][1, rows].astype(F32)
            cdf, density = gelu_parts(hidden)
            act[rows, summed(n, h)] = (hidden * cdf).astype(BF16)
            grad = cot[rows, summed(n, h)].astype(F32) * (cdf + hidden * density)
            grad = grad.astype(BF16)
            width = grad.shape[-1]
            if h == 0:
                g[n, 0, slot(0, 0, 0), rows, 0 : min(width, fh)] = grad[:, 0 : min(width, fh)]
                if width > fh:
                    g[n, 1, slot(1, 0, 0), rows, 0 : width - fh] = grad[:, fh:width]
            else:
                g[n, 1, slot(1, 0, 0), rows, fh - width : fh] = grad

    def block(c, h, j, i):
        n, start, size, _ = GATHERS[c]
        return g.at[n, h, slot(h, j, i), pl.ds(start, size)]

    def share(c, h, j, i, axis, delta):
        n, start, size, straight = GATHERS[c]
        axis_a = ring(h)[0]
        nj, ni = (j, (i - delta) % SIDE) if axis == axis_a else ((j - delta) % SIDE, i)
        ref = block(c, h, j, i)
        if delta != 2 and 2 in (ni if axis == axis_a else nj,):
            ref = g.at[n, h, slot(h, j, i), pl.ds(start if delta == 1 else start + size // 2, size // 2)]
        push(ref, ref, g_send.at[c, h], g_sem.at[c, h, nj, ni], grid_device(axis, delta))

    def ways(c):
        return (1, -1, 2) if GATHERS[c][3] else (1, -1)

    here = set()

    def block_here(c, h, j, i):
        if (c, h, j, i) not in here:
            here.add((c, h, j, i))
            arrived(block(c, h, j, i), g_sem.at[c, h, j, i])

    def task_s(c, h):
        axis_a, axis_b, _, _ = ring(h)
        here.add((c, h, 0, 0))
        for axis in (axis_b, axis_a):
            for delta in ways(c):
                share(c, h, 0, 0, axis, delta)

    def task_a1(c, h):
        axis_a, axis_b, _, _ = ring(h)
        for j, delta in ((3, 1), (1, -1)):
            block_here(c, h, j, 0)
            if not GATHERS[c][3]:
                share(c, h, j, 0, axis_b, delta)
        for j in (3, 1):
            for delta in ways(c):
                share(c, h, j, 0, axis_a, delta)

    def task_a2(c, h):
        axis_a = ring(h)[0]
        block_here(c, h, 2, 0)
        for delta in ways(c):
            share(c, h, 2, 0, axis_a, delta)

    def task_a(c, h, step):
        if step == 1:
            task_a1(c, h)
        else:
            task_a2(c, h)

    def task_b(c, h, j):
        axis_a = ring(h)[0]
        if not GATHERS[c][3]:
            block_here(c, h, j, 3)
            share(c, h, j, 3, axis_a, 1)
            block_here(c, h, j, 1)
            share(c, h, j, 1, axis_a, -1)

    finished = set()

    def task_t(c, h, i):
        n, start, size, _ = GATHERS[c]
        rows = pl.ds(start, size)
        at_x = (yx[1] + i) % SIDE
        for k in range(SIDE):
            block_here(c, h, *((k, i) if h == 0 else (i, k)))
        if h == 0:
            blocks = jnp.concatenate([g[n, h, SIDE * at_y + at_x, rows] for at_y in range(SIDE)], axis=0)
        else:
            blocks = g[n, h, pl.ds(SIDE * at_x, SIDE), rows].reshape(SIDE * size, fh)
        terms = lax.dot_general(
            blocks, w[:, columns(n, h)], (((1,), (1,)), ((), ())), preferred_element_type=F32
        )
        for at_y in range(SIDE):
            at = SIDE * at_y + at_x
            gt[at, rows] = gt[at, rows] + terms[size * at_y : size * at_y + size]
        finished.add((c, h, i))
        if n == NCH - 1 and (c, 1 - h, i) in finished:
            for at_y in range(SIDE):
                send_tokens(SIDE * at_y + at_x, rows)

    def send_tokens(at, rows):
        zsend[at, rows] = gt[at, rows].astype(BF16)
        to = at // 2
        ahead = (to - row + ROWS) % ROWS

        @pl.when(ahead != 0)
        def _():
            place = ROWS - 1 - ahead
            push(zsend.at[at, rows], zrecv.at[place, at % 2, rows], zs_send.at[0], zs_recv.at[0], {"row": to})

    def task_w(c, h):
        n, start, size, _ = GATHERS[c]
        for j in range(SIDE):
            for i in range(SIDE):
                block_here(c, h, j, i)
        total = None
        for t in range(start // half, (start + size) // half):
            rows = g[n, h, :, pl.ds(half * t, half)].reshape(512, fh)
            term = jnp.dot(tok_t[h, t], rows, preferred_element_type=F32)
            total = term if total is None else total + term
        if start > 0:
            total = gw[n, h] + total
        if start + size < 64:
            gw[n, h] = total
        else:
            gwb[n, h] = total.astype(BF16)
            cols = columns(n, h)
            push(gwb.at[n, h], other_hbm.at[:, cols], dep_send.at[n, h], dep_recv.at[n, h], other)
            pltpu.make_async_copy(gwb.at[n, h], own_hbm.at[:, cols], out_sem.at[n, h]).start()

    by_half = {
        "I": task_i, "F": task_f, "D": task_d, "G": task_f2, "H": task_d2,
        "S": task_s, "A": task_a, "B": task_b, "T": task_t, "W": task_w,
    }
    without_step = "GHSW"
    cot_waited = False
    for name, n, j in ORDER:
        if name[0] == "H" and not cot_waited:
            loads[2].wait()
            cot_waited = True
        if name == "Z":
            task_z(j)
        elif name == "IW":
            task_iw(n, j)
        elif name == "FP":
            task_f(n, 0, (waves[j] - yx[0] + SIDE) % SIDE)
        elif name == "DP":
            task_dp(n, j)
        elif name == "tokens":
            task_tokens()
        elif name == "transposes":
            task_transposes()
        elif name[0] in without_step:
            by_half[name[0]](n, int(name[1]))
        else:
            by_half[name[0]](n, int(name[1]), j)

    act_out = pltpu.make_async_copy(act, act_hbm, local_sem.at[0])
    act_out.start()
    arrived(zrecv, zs_recv.at[0])
    for at in range(2):
        total = gt[2 * row + at].astype(BF16).astype(F32)
        for place in range(ROWS - 1):
            total = total + zrecv[place, at].astype(F32)
        zsend[2 * row + at] = total.astype(BF16)
    gt_out = pltpu.make_async_copy(zsend.at[pl.ds(2 * row, 2)], gt_hbm, local_sem.at[1])
    gt_out.start()

    for n in range(NCH):
        for h in (0, 1):
            sent(r1[n][h], send.at[n, h, 0])
            sent(s[n][h], send.at[n, h, 1])
            sent(s[n][h].at[pl.ds(0, 3)], send.at[n, h, 2])
            cols = columns(n, h)
            pltpu.make_async_copy(gwb.at[n, h], own_hbm.at[:, cols], out_sem.at[n, h]).wait()
            done = remote(gwb.at[n, h], other_hbm.at[:, cols], dep_send.at[n, h], dep_recv.at[n, h], other)
            done.wait_send()
            done.wait_recv()
    for c, (n, start, size, _) in enumerate(GATHERS):
        for h in (0, 1):
            sent(g.at[n, h, pl.ds(0, 15), pl.ds(start, size)], g_send.at[c, h])
    for delta in range(4):
        for k in (0, 1):
            for way in (0, 1):
                if delta < 3 or k == way:
                    sent(tok.at[0, 0], z_send.at[4 * delta + 2 * k + way])
    sent(zsend.at[pl.ds(0, 14)], zs_send.at[0])
    act_out.wait()
    gt_out.wait()


def local(tokens, weight, cotangent):
    d, f = weight.shape
    fh = f // (2 * NCH)
    any_spec = pl.BlockSpec(memory_space=pl.ANY)
    vmem = pltpu.VMEM
    dma = pltpu.SemaphoreType.DMA

    def halves(*shape):
        return tuple(
            tuple(vmem(shape + (2 * fh * part // 4,), BF16) for part in (share, 4 - share)) for share in X_FIRST
        )

    act, own, other, gt = pl.pallas_call(
        kernel,
        out_shape=(
            jax.ShapeDtypeStruct(cotangent.shape, BF16),
            jax.ShapeDtypeStruct(weight.shape, BF16),
            jax.ShapeDtypeStruct(weight.shape, BF16),
            jax.ShapeDtypeStruct((2, 64, d), BF16),
        ),
        in_specs=[any_spec] * 3,
        out_specs=(any_spec,) * 4,
        scratch_shapes=[
            vmem(weight.shape, BF16),
            vmem(cotangent.shape, BF16),
            vmem(cotangent.shape, BF16),
            vmem((2, 16, 64, d), BF16),
            vmem((2, 2, d, 512), BF16),
            halves(16, 64),
            halves(SIDE, 2, 32),
            halves(SIDE, 2, 64),
            halves(SIDE, 64),
            halves(2, 32),
            halves(2, 64),
            vmem((NCH, 2, 16, 64, fh), BF16),
            vmem((NCH, 2, d, fh), F32),
            vmem((NCH, 2, d, fh), BF16),
            vmem((16, 64, d), F32),
            vmem((16, 64, d), BF16),
            vmem((ROWS - 1, 2, 64, d), BF16),
            dma((3,)),
            dma((NCH, 2)),
            dma((16,)),
            dma((16,)),
            dma((NCH, 2, 3)),
            dma((len(GATHERS), 2)),
            dma((NCH, 2, SIDE, 2)),
            dma((NCH, 2, SIDE)),
            dma((NCH, 2)),
            dma((NCH, 2)),
            dma((len(GATHERS), 2, SIDE, SIDE)),
            dma((NCH, 2)),
            dma((NCH, 2)),
            dma((1,)),
            dma((1,)),
        ],
        compiler_params=pltpu.CompilerParams(
            collective_id=0, has_side_effects=True, vmem_limit_bytes=48 * 2**20
        ),
    )(tokens.reshape(2, 64, d), weight, cotangent)
    grad_weight = (own.astype(F32) + other.astype(F32)).astype(BF16)
    return (act, gt.reshape(128, d), grad_weight)


def solution(mesh):
    placed = (P(("depth", "row"), "col"), P("col", "row"), P(("depth", "col"), "row"))
    return jax.shard_map(
        local,
        mesh=mesh,
        in_specs=placed,
        out_specs=(P(("depth", "col"), "row"), P(("depth", "row"), "col"), P("col", "row")),
        check_vma=False,
    )
```

```python
import functools
import math

import jax
import jax.numpy as jnp
from jax import lax
from jax.experimental import pallas as pl
from jax.experimental.pallas import tpu as pltpu
from jax.sharding import PartitionSpec as P

MESH = pl.DeviceIdType.MESH
NCH = 2
X_FIRST = (8, 6)
SIDE = 4
ROWS = 8
BF16 = jnp.bfloat16
F32 = jnp.float32


def gelu_parts(hidden):
    cdf = 0.5 * (1.0 + lax.erf(hidden * (1.0 / math.sqrt(2.0))))
    density = jnp.exp(-0.5 * hidden * hidden) * (1.0 / math.sqrt(2.0 * math.pi))
    return (cdf, density)


GATHERS = ((0, 0, 64, False), (1, 0, 64, False))


ORDER = (
    ("Z", 0, 1), ("IW", 0, 0), ("FP", 0, 0), ("Z", 0, 2), ("IW", 0, 1), ("DP", 0, 0), ("FP", 0, 1),
    ("Z", 0, 3), ("Z", 0, 4), ("IW", 0, 2), ("IW", 0, 3), ("FQ", 0, 1), ("tokens", 0, 0), ("DP", 0, 1),
    ("I0", 1, 0), ("I0", 1, 1), ("I0", 1, 2), ("FP", 0, 2), ("I0", 1, 3), ("I1", 1, 0), ("I1", 1, 1),
    ("I1", 1, 2), ("I1", 1, 3), ("transposes", 0, 0), ("FP", 0, 3), ("FQ", 0, 0), ("F0", 1, 0), ("F1", 1, 0),
    ("F0", 1, 1), ("F1", 1, 1), ("F0", 1, 2), ("F1", 1, 2), ("D1", 0, 0), ("DP", 0, 2), ("D1", 0, 1),
    ("F0", 1, 3), ("D1", 0, 2), ("F1", 1, 3), ("D1", 0, 3), ("D1", 1, 0), ("DP", 0, 3), ("D1", 1, 1),
    ("D0", 1, 0), ("D1", 1, 2), ("D0", 1, 1), ("D0", 1, 2), ("D1", 1, 3), ("D0", 1, 3), ("G0", 0, 0),
    ("G1", 0, 0), ("G0", 1, 0), ("G1", 1, 0), ("H1", 0, 0), ("H0", 0, 0), ("S0", 0, 0), ("S1", 0, 0),
    ("H0", 1, 0), ("H1", 1, 0), ("S0", 1, 0), ("S1", 1, 0), ("A0", 0, 1), ("B0", 0, 0), ("B1", 0, 0),
    ("A1", 0, 1), ("A0", 1, 1), ("B0", 1, 0), ("B1", 1, 0), ("A1", 1, 1), ("A0", 0, 2), ("T0", 0, 0),
    ("T1", 0, 0), ("B0", 0, 3), ("B1", 0, 3), ("B0", 0, 1), ("B1", 0, 1), ("A1", 0, 2), ("A0", 1, 2),
    ("T0", 1, 0), ("T1", 1, 0), ("B0", 1, 3), ("B1", 1, 3), ("B0", 1, 1), ("B1", 1, 1), ("A1", 1, 2),
    ("T1", 0, 3), ("T1", 0, 1), ("B0", 0, 2), ("T0", 0, 1), ("T0", 0, 3), ("B1", 0, 2), ("T1", 1, 3),
    ("T1", 1, 1), ("B0", 1, 2), ("T0", 1, 1), ("T0", 1, 3), ("B1", 1, 2), ("T1", 0, 2), ("T0", 0, 2),
    ("W0", 0, 0), ("T0", 1, 2), ("T1", 1, 2), ("W1", 0, 0), ("W0", 1, 0), ("W1", 1, 0),
)


def kernel(
    tok_hbm, w_hbm, cot_hbm, act_hbm, own_hbm, other_hbm, gt_hbm,
    w, cot, act, tok, tok_t, part, f1, r1, s, f2, r2, g, gw, gwb, gt, zsend, zrecv,
    local_sem, out_sem, z_send, z_recv, send, g_send, f1_sem, r1_sem, f2_sem, r2_sem, g_sem,
    dep_send, dep_recv, zs_send, zs_recv,
):
    fh = g.shape[-1]
    half = 32
    depth, row, col = (lax.axis_index(a) for a in ("depth", "row", "col"))
    yx = (col // SIDE, col % SIDE)
    lo, hi = pl.ds(0, half), pl.ds(half, half)

    loads = [
        pltpu.make_async_copy(tok_hbm, tok.at[0, pl.ds(2 * row, 2)], local_sem.at[0]),
        pltpu.make_async_copy(w_hbm, w, local_sem.at[1]),
        pltpu.make_async_copy(cot_hbm, cot, local_sem.at[2]),
    ]
    for load in loads:
        load.start()

    def grid_device(axis, delta):
        at = list(yx)
        at[axis] = (at[axis] + delta + SIDE) % SIDE
        return {"col": at[0] * SIDE + at[1]}

    def row_device(delta):
        return {"row": (row + delta + ROWS) % ROWS}

    other = {"depth": 1 - depth}

    barrier = pltpu.get_barrier_semaphore()
    peers = [row_device(d) for d in range(1, ROWS)]
    peers += [grid_device(axis, delta) for axis in (0, 1) for delta in (1, 2, 3)]
    peers += [other]
    for peer in peers:
        pl.semaphore_signal(barrier, inc=1, device_id=peer, device_id_type=MESH)
    loads[0].wait()
    pl.semaphore_wait(barrier, len(peers))

    def remote(src, dst, ssem, rsem, device):
        return pltpu.make_async_remote_copy(
            src_ref=src, dst_ref=dst, send_sem=ssem, recv_sem=rsem,
            device_id=device, device_id_type=MESH,
        )

    def push(src, dst, ssem, rsem, device):
        remote(src, dst, ssem, rsem, device).start()

    def arrived(ref, rsem):
        remote(ref, ref, send.at[0, 0, 0], rsem, other).wait_recv()

    def sent(ref, ssem):
        remote(ref, ref, ssem, f2_sem.at[0, 0], other).wait_send()

    def piece(delta, k):
        return tok.at[0, 2 * ((row + delta + ROWS) % ROWS) + k]

    def hand_on(delta, k, way, far=1):
        sem = 4 * (abs(delta) + far - 1) + 2 * k + way
        device = row_device(far * (1 - 2 * way))
        push(piece(delta, k), piece(delta, k), z_send.at[sem], z_recv.at[sem], device)

    for k in (0, 1):
        hand_on(0, k, 0)
        hand_on(0, k, 1)
    gt[...] = jnp.zeros_like(gt)

    def task_z(step):
        for k in (0, 1):
            for way in (0, 1):
                if step == 4 and k != way:
                    continue
                delta = -step if way == 0 else step
                arrived(piece(delta, k), z_recv.at[4 * (step - 1) + 2 * k + way])
                if step < 3:
                    hand_on(delta, k, way)
                if step == 2 and k == way:
                    hand_on(delta, k, way, 2)

    def task_tokens():
        for at_y in range(SIDE):
            for at_x in range(SIDE):
                tok[1, at_x * SIDE + at_y] = tok[0, at_y * SIDE + at_x]

    def task_transposes():
        for h in range(2):
            for t in range(2):
                tok_t[h, t] = tok[h, :, pl.ds(32 * t, 32)].reshape(512, 384).T

    def ring(h):
        axis_a, axis_b = (1, 0) if h == 0 else (0, 1)
        return axis_a, axis_b, yx[axis_a], yx[axis_b]

    def slot(h, j, i):
        _, _, a, b = ring(h)
        return ((b + j) % SIDE) * SIDE + (a + i) % SIDE

    def columns(n, h):
        return pl.ds((2 * n + h) * fh, fh)

    def summed(n, h):
        width = part[n][h].shape[-1]
        return pl.ds(2 * n * fh + (0 if h == 0 else 2 * fh - width), width)

    def group(h, j):
        _, _, _, b = ring(h)
        return (b + j) % SIDE

    toward = 1 - 2 * (row % 2)
    waves = [row // 2, (row // 2 - toward + SIDE) % SIDE, (row // 2 + toward + SIDE) % SIDE, (row // 2 + 2) % SIDE]

    def first_sends(n, h, j):
        axis_a = ring(h)[0]
        right, left = grid_device(axis_a, 1), grid_device(axis_a, -1)
        ssem = send.at[n, h, 0]
        far = part[n][h].at[slot(h, j, 2)]
        push(far.at[lo], f1[n][h].at[j, 0], ssem, f1_sem.at[n, h, j, 0], right)
        push(far.at[hi], f1[n][h].at[j, 1], ssem, f1_sem.at[n, h, j, 1], left)
        push(part[n][h].at[slot(h, j, 1), hi], r1[n][h].at[j, 0, hi], ssem, r1_sem.at[n, h, j], right)
        push(part[n][h].at[slot(h, j, 3), lo], r1[n][h].at[j, 1, lo], ssem, r1_sem.at[n, h, j], left)

    def task_iw(n, wave):
        if wave == 0:
            loads[1].wait()
        at_y = waves[wave]
        role = (at_y - yx[0] + SIDE) % SIDE
        task_i(n, 0, role)
        x = tok[0, pl.ds(SIDE * at_y, SIDE)].reshape(256, 384)
        y = jnp.dot(x, w[:, summed(n, 1)], preferred_element_type=F32).astype(BF16)
        for at_x in range(SIDE):
            part[n][1][SIDE * at_x + at_y] = y[64 * at_x : 64 * at_x + 64]
        right, left = grid_device(0, 1), grid_device(0, -1)
        ssem = send.at[n, 1, 0]

        @pl.when(role == 2)
        def _():
            for j in range(SIDE):
                far = part[n][1].at[slot(1, j, 2)]
                push(far.at[lo], f1[n][1].at[j, 0], ssem, f1_sem.at[n, 1, j, 0], right)
                push(far.at[hi], f1[n][1].at[j, 1], ssem, f1_sem.at[n, 1, j, 1], left)

        @pl.when(role == 1)
        def _():
            for j in range(SIDE):
                push(part[n][1].at[slot(1, j, 1), hi], r1[n][1].at[j, 0, hi], ssem, r1_sem.at[n, 1, j], right)

        @pl.when(role == 3)
        def _():
            for j in range(SIDE):
                push(part[n][1].at[slot(1, j, 3), lo], r1[n][1].at[j, 1, lo], ssem, r1_sem.at[n, 1, j], left)

    def task_i(n, h, j):
        four = pl.ds(SIDE * group(h, j), SIDE)
        x = tok[h, four].reshape(256, 384)
        y = jnp.dot(x, w[:, summed(n, h)], preferred_element_type=F32).astype(BF16)
        part[n][h][four] = y.reshape(SIDE, 64, y.shape[-1])
        first_sends(n, h, j)

    def forward(n, h, j, way):
        axis_a = ring(h)[0]
        device = grid_device(axis_a, 1 - 2 * way)
        rows, near = (lo, 1) if way == 0 else (hi, 3)
        arrived(f1[n][h].at[j, way], f1_sem.at[n, h, j, way])
        f1[n][h][j, way] = (
            f1[n][h][j, way].astype(F32) + part[n][h][slot(h, j, near), rows].astype(F32)
        ).astype(BF16)
        push(f1[n][h].at[j, way], r1[n][h].at[j, way, rows], send.at[n, h, 1], r1_sem.at[n, h, j], device)

    def task_f(n, h, j):
        forward(n, h, j, 0)
        forward(n, h, j, 1)

    def sum_first(n, h, j):
        arrived(r1[n][h].at[j], r1_sem.at[n, h, j])
        total = part[n][h][slot(h, j, 0)].astype(F32)
        total = total + r1[n][h][j, 0].astype(F32) + r1[n][h][j, 1].astype(F32)
        s[n][h][j] = total.astype(BF16)

    def second_sends(n, h, j):
        axis_b = ring(h)[1]
        right, left = grid_device(axis_b, 1), grid_device(axis_b, -1)
        ssem = send.at[n, h, 2]
        if j == 2:
            push(s[n][h].at[2, lo], f2[n][h].at[0], ssem, f2_sem.at[n, h], right)
            push(s[n][h].at[2, hi], f2[n][h].at[1], ssem, f2_sem.at[n, h], left)
        elif j == 1:
            push(s[n][h].at[1, hi], r2[n][h].at[0, hi], ssem, r2_sem.at[n, h], right)
        elif j == 3:
            push(s[n][h].at[3, lo], r2[n][h].at[1, lo], ssem, r2_sem.at[n, h], left)

    def task_d(n, h, j):
        sum_first(n, h, j)
        second_sends(n, h, j)

    def task_dp(n, wave):
        j = (waves[wave] - yx[0] + SIDE) % SIDE
        sum_first(n, 0, j)
        for role in (1, 2, 3):
            pl.when(j == role)(functools.partial(second_sends, n, 0, role))

    def task_f2(n, h):
        axis_b = ring(h)[1]
        right, left = grid_device(axis_b, 1), grid_device(axis_b, -1)
        ssem = send.at[n, h, 2]
        arrived(f2[n][h], f2_sem.at[n, h])
        f2[n][h][0] = (f2[n][h][0].astype(F32) + s[n][h][1, lo].astype(F32)).astype(BF16)
        push(f2[n][h].at[0], r2[n][h].at[0, lo], ssem, r2_sem.at[n, h], right)
        f2[n][h][1] = (f2[n][h][1].astype(F32) + s[n][h][3, hi].astype(F32)).astype(BF16)
        push(f2[n][h].at[1], r2[n][h].at[1, hi], ssem, r2_sem.at[n, h], left)

    def task_d2(n, h):
        arrived(r2[n][h], r2_sem.at[n, h])

        @pl.loop(0, 4)
        def _(at):
            rows = pl.ds(pl.multiple_of(at * 16, 16), 16)
            hidden = s[n][h][0, rows].astype(F32) + r2[n][h][0, rows].astype(F32) + r2[n][h][1, rows].astype(F32)
            cdf, density = gelu_parts(hidden)
            act[rows, summed(n, h)] = (hidden * cdf).astype(BF16)
            grad = cot[rows, summed(n, h)].astype(F32) * (cdf + hidden * density)
            grad = grad.astype(BF16)
            width = grad.shape[-1]
            if h == 0:
                g[n, 0, slot(0, 0, 0), rows, 0 : min(width, fh)] = grad[:, 0 : min(width, fh)]
                if width > fh:
                    g[n, 1, slot(1, 0, 0), rows, 0 : width - fh] = grad[:, fh:width]
            else:
                g[n, 1, slot(1, 0, 0), rows, fh - width : fh] = grad

    def block(c, h, j, i):
        n, start, size, _ = GATHERS[c]
        return g.at[n, h, slot(h, j, i), pl.ds(start, size)]

    def share(c, h, j, i, axis, delta):
        n, start, size, straight = GATHERS[c]
        axis_a = ring(h)[0]
        nj, ni = (j, (i - delta) % SIDE) if axis == axis_a else ((j - delta) % SIDE, i)
        ref = block(c, h, j, i)
        if delta != 2 and 2 in (ni if axis == axis_a else nj,):
            ref = g.at[n, h, slot(h, j, i), pl.ds(start if delta == 1 else start + size // 2, size // 2)]
        push(ref, ref, g_send.at[c, h], g_sem.at[c, h, nj, ni], grid_device(axis, delta))

    def ways(c):
        return (1, -1, 2) if GATHERS[c][3] else (1, -1)

    here = set()

    def block_here(c, h, j, i):
        if (c, h, j, i) not in here:
            here.add((c, h, j, i))
            arrived(block(c, h, j, i), g_sem.at[c, h, j, i])

    def task_s(c, h):
        axis_a, axis_b, _, _ = ring(h)
        here.add((c, h, 0, 0))
        for axis in (axis_b, axis_a):
            for delta in ways(c):
                share(c, h, 0, 0, axis, delta)

    def task_a1(c, h):
        axis_a, axis_b, _, _ = ring(h)
        for j, delta in ((3, 1), (1, -1)):
            block_here(c, h, j, 0)
            if not GATHERS[c][3]:
                share(c, h, j, 0, axis_b, delta)
        for j in (3, 1):
            for delta in ways(c):
                share(c, h, j, 0, axis_a, delta)

    def task_a2(c, h):
        axis_a = ring(h)[0]
        block_here(c, h, 2, 0)
        for delta in ways(c):
            share(c, h, 2, 0, axis_a, delta)

    def task_a(c, h, step):
        if step == 1:
            task_a1(c, h)
        else:
            task_a2(c, h)

    def task_b(c, h, j):
        axis_a = ring(h)[0]
        if not GATHERS[c][3]:
            block_here(c, h, j, 3)
            share(c, h, j, 3, axis_a, 1)
            block_here(c, h, j, 1)
            share(c, h, j, 1, axis_a, -1)

    finished = set()

    def task_t(c, h, i):
        n, start, size, _ = GATHERS[c]
        rows = pl.ds(start, size)
        at_x = (yx[1] + i) % SIDE
        for k in range(SIDE):
            block_here(c, h, *((k, i) if h == 0 else (i, k)))
        if h == 0:
            blocks = jnp.concatenate([g[n, h, SIDE * at_y + at_x, rows] for at_y in range(SIDE)], axis=0)
        else:
            blocks = g[n, h, pl.ds(SIDE * at_x, SIDE), rows].reshape(SIDE * size, fh)
        terms = lax.dot_general(
            blocks, w[:, columns(n, h)], (((1,), (1,)), ((), ())), preferred_element_type=F32
        )
        for at_y in range(SIDE):
            at = SIDE * at_y + at_x
            gt[at, rows] = gt[at, rows] + terms[size * at_y : size * at_y + size]
        finished.add((c, h, i))
        if n == NCH - 1 and (c, 1 - h, i) in finished:
            for at_y in range(SIDE):
                send_tokens(SIDE * at_y + at_x, rows)

    def send_tokens(at, rows):
        zsend[at, rows] = gt[at, rows].astype(BF16)
        to = at // 2
        ahead = (to - row + ROWS) % ROWS

        @pl.when(ahead != 0)
        def _():
            place = ROWS - 1 - ahead
            push(zsend.at[at, rows], zrecv.at[place, at % 2, rows], zs_send.at[0], zs_recv.at[0], {"row": to})

    def task_w(c, h):
        n, start, size, _ = GATHERS[c]
        for j in range(SIDE):
            for i in range(SIDE):
                block_here(c, h, j, i)
        total = None
        for t in range(start // half, (start + size) // half):
            rows = g[n, h, :, pl.ds(half * t, half)].reshape(512, fh)
            term = jnp.dot(tok_t[h, t], rows, preferred_element_type=F32)
            total = term if total is None else total + term
        if start > 0:
            total = gw[n, h] + total
        if start + size < 64:
            gw[n, h] = total
        else:
            gwb[n, h] = total.astype(BF16)
            cols = columns(n, h)
            push(gwb.at[n, h], other_hbm.at[:, cols], dep_send.at[n, h], dep_recv.at[n, h], other)
            pltpu.make_async_copy(gwb.at[n, h], own_hbm.at[:, cols], out_sem.at[n, h]).start()

    by_half = {
        "I": task_i, "F": task_f, "D": task_d, "G": task_f2, "H": task_d2,
        "S": task_s, "A": task_a, "B": task_b, "T": task_t, "W": task_w,
    }
    without_step = "GHSW"
    cot_waited = False
    for name, n, j in ORDER:
        if name[0] == "H" and not cot_waited:
            loads[2].wait()
            cot_waited = True
        if name == "Z":
            task_z(j)
        elif name == "IW":
            task_iw(n, j)
        elif name == "FP":
            task_f(n, 0, (waves[j] - yx[0] + SIDE) % SIDE)
        elif name == "FQ":
            for k in range(SIDE):
                forward(n, 1, k, j)
        elif name == "DP":
            task_dp(n, j)
        elif name == "tokens":
            task_tokens()
        elif name == "transposes":
            task_transposes()
        elif name[0] in without_step:
            by_half[name[0]](n, int(name[1]))
        else:
            by_half[name[0]](n, int(name[1]), j)

    act_out = pltpu.make_async_copy(act, act_hbm, local_sem.at[0])
    act_out.start()
    arrived(zrecv, zs_recv.at[0])
    for at in range(2):
        total = gt[2 * row + at].astype(BF16).astype(F32)
        for place in range(ROWS - 1):
            total = total + zrecv[place, at].astype(F32)
        zsend[2 * row + at] = total.astype(BF16)
    gt_out = pltpu.make_async_copy(zsend.at[pl.ds(2 * row, 2)], gt_hbm, local_sem.at[1])
    gt_out.start()

    for n in range(NCH):
        for h in (0, 1):
            sent(r1[n][h], send.at[n, h, 0])
            sent(s[n][h], send.at[n, h, 1])
            sent(s[n][h].at[pl.ds(0, 3)], send.at[n, h, 2])
            cols = columns(n, h)
            pltpu.make_async_copy(gwb.at[n, h], own_hbm.at[:, cols], out_sem.at[n, h]).wait()
            done = remote(gwb.at[n, h], other_hbm.at[:, cols], dep_send.at[n, h], dep_recv.at[n, h], other)
            done.wait_send()
            done.wait_recv()
    for c, (n, start, size, _) in enumerate(GATHERS):
        for h in (0, 1):
            sent(g.at[n, h, pl.ds(0, 15), pl.ds(start, size)], g_send.at[c, h])
    for delta in range(4):
        for k in (0, 1):
            for way in (0, 1):
                if delta < 3 or k == way:
                    sent(tok.at[0, 0], z_send.at[4 * delta + 2 * k + way])
    sent(zsend.at[pl.ds(0, 14)], zs_send.at[0])
    act_out.wait()
    gt_out.wait()


def finish(own, other, act, gt, gw_out, act_out, gt_out, total, sem):
    copies = [pltpu.make_async_copy(act, act_out, sem.at[6]), pltpu.make_async_copy(gt, gt_out, sem.at[7])]
    for copy in copies:
        copy.start()
    step = own.shape[0] // 6
    for k in range(6):
        rows = pl.ds(k * step, step)
        total[rows] = (own[rows].astype(F32) + other[rows].astype(F32)).astype(BF16)
        copies.append(pltpu.make_async_copy(total.at[rows], gw_out.at[rows], sem.at[k]))
        copies[-1].start()
    for copy in copies:
        copy.wait()


def local(tokens, weight, cotangent):
    d, f = weight.shape
    fh = f // (2 * NCH)
    any_spec = pl.BlockSpec(memory_space=pl.ANY)
    vmem = pltpu.VMEM
    dma = pltpu.SemaphoreType.DMA

    def halves(*shape):
        return tuple(
            tuple(vmem(shape + (2 * fh * part // 12,), BF16) for part in (share, 12 - share)) for share in X_FIRST
        )

    act, own, other, gt = pl.pallas_call(
        kernel,
        out_shape=(
            jax.ShapeDtypeStruct(cotangent.shape, BF16),
            jax.ShapeDtypeStruct(weight.shape, BF16),
            jax.ShapeDtypeStruct(weight.shape, BF16),
            jax.ShapeDtypeStruct((2, 64, d), BF16),
        ),
        in_specs=[any_spec] * 3,
        out_specs=(any_spec,) * 4,
        scratch_shapes=[
            vmem(weight.shape, BF16),
            vmem(cotangent.shape, BF16),
            vmem(cotangent.shape, BF16),
            vmem((2, 16, 64, d), BF16),
            vmem((2, 2, d, 512), BF16),
            halves(16, 64),
            halves(SIDE, 2, 32),
            halves(SIDE, 2, 64),
            halves(SIDE, 64),
            halves(2, 32),
            halves(2, 64),
            vmem((NCH, 2, 16, 64, fh), BF16),
            vmem((NCH, 2, d, fh), F32),
            vmem((NCH, 2, d, fh), BF16),
            vmem((16, 64, d), F32),
            vmem((16, 64, d), BF16),
            vmem((ROWS - 1, 2, 64, d), BF16),
            dma((3,)),
            dma((NCH, 2)),
            dma((16,)),
            dma((16,)),
            dma((NCH, 2, 3)),
            dma((len(GATHERS), 2)),
            dma((NCH, 2, SIDE, 2)),
            dma((NCH, 2, SIDE)),
            dma((NCH, 2)),
            dma((NCH, 2)),
            dma((len(GATHERS), 2, SIDE, SIDE)),
            dma((NCH, 2)),
            dma((NCH, 2)),
            dma((1,)),
            dma((1,)),
        ],
        compiler_params=pltpu.CompilerParams(
            collective_id=0, has_side_effects=True, vmem_limit_bytes=48 * 2**20
        ),
    )(tokens.reshape(2, 64, d), weight, cotangent)
    grad_weight, act, gt = pl.pallas_call(
        finish,
        out_shape=(
            jax.ShapeDtypeStruct(weight.shape, BF16),
            jax.ShapeDtypeStruct(cotangent.shape, BF16),
            jax.ShapeDtypeStruct((2, 64, d), BF16),
        ),
        in_specs=[pl.BlockSpec(memory_space=vmem)] * 4,
        out_specs=(pl.BlockSpec(memory_space=pltpu.HBM),) * 3,
        scratch_shapes=[vmem(weight.shape, BF16), dma((8,))],
        compiler_params=pltpu.CompilerParams(vmem_limit_bytes=8 * 2**20),
    )(own, other, act, gt)
    return (act, gt.reshape(128, d), grad_weight)


def solution(mesh):
    placed = (P(("depth", "row"), "col"), P("col", "row"), P(("depth", "col"), "row"))
    return jax.shard_map(
        local,
        mesh=mesh,
        in_specs=placed,
        out_specs=(P(("depth", "col"), "row"), P(("depth", "row"), "col"), P("col", "row")),
        check_vma=False,
    )
```

```python
import functools
import math

import jax
import jax.numpy as jnp
from jax import lax
from jax.experimental import pallas as pl
from jax.experimental.pallas import tpu as pltpu
from jax.sharding import PartitionSpec as P

MESH = pl.DeviceIdType.MESH
NCH = 2
X_FIRST = (8, 6)
SIDE = 4
ROWS = 8
BF16 = jnp.bfloat16
F32 = jnp.float32


def gelu_parts(hidden):
    cdf = 0.5 * (1.0 + lax.erf(hidden * (1.0 / math.sqrt(2.0))))
    density = jnp.exp(-0.5 * hidden * hidden) * (1.0 / math.sqrt(2.0 * math.pi))
    return (cdf, density)


GATHERS = ((0, 0, 64, False), (1, 0, 64, False))


ORDER = (
    ("Z", 0, 1), ("IW", 0, 0), ("FP", 0, 0), ("Z", 0, 2), ("IW", 0, 1), ("DP", 0, 0), ("FP", 0, 1),
    ("Z", 0, 3), ("Z", 0, 4), ("IW", 0, 2), ("IW", 0, 3), ("FQ", 0, 1), ("tokens", 0, 0), ("DP", 0, 1),
    ("I0", 1, 0), ("I0", 1, 1), ("I0", 1, 2), ("FP", 0, 2), ("I0", 1, 3), ("I1", 1, 0), ("I1", 1, 1),
    ("I1", 1, 2), ("I1", 1, 3), ("transposes", 0, 0), ("FP", 0, 3), ("FQ", 0, 0), ("F0", 1, 0), ("F1", 1, 0),
    ("F0", 1, 1), ("F1", 1, 1), ("F0", 1, 2), ("F1", 1, 2), ("D1", 0, 0), ("DP", 0, 2), ("D1", 0, 1),
    ("F0", 1, 3), ("D1", 0, 2), ("F1", 1, 3), ("D1", 0, 3), ("D1", 1, 0), ("DP", 0, 3), ("D1", 1, 1),
    ("D0", 1, 0), ("D1", 1, 2), ("D0", 1, 1), ("D0", 1, 2), ("D1", 1, 3), ("D0", 1, 3), ("G0", 0, 0),
    ("G1", 0, 0), ("G0", 1, 0), ("G1", 1, 0), ("H1", 0, 0), ("H0", 0, 0), ("S0", 0, 0), ("S1", 0, 0),
    ("H0", 1, 0), ("H1", 1, 0), ("S0", 1, 0), ("S1", 1, 0), ("A0", 0, 1), ("B0", 0, 0), ("B1", 0, 0),
    ("A1", 0, 1), ("A0", 1, 1), ("B0", 1, 0), ("B1", 1, 0), ("A1", 1, 1), ("A0", 0, 2), ("T0", 0, 0),
    ("T1", 0, 0), ("B0", 0, 3), ("B1", 0, 3), ("B0", 0, 1), ("B1", 0, 1), ("A1", 0, 2), ("A0", 1, 2),
    ("T0", 1, 0), ("T1", 1, 0), ("B0", 1, 3), ("B1", 1, 3), ("B0", 1, 1), ("B1", 1, 1), ("A1", 1, 2),
    ("T1", 0, 3), ("T1", 0, 1), ("B0", 0, 2), ("T0", 0, 1), ("T0", 0, 3), ("B1", 0, 2), ("T1", 1, 3),
    ("T1", 1, 1), ("B0", 1, 2), ("T0", 1, 1), ("T0", 1, 3), ("B1", 1, 2), ("T1", 0, 2), ("T0", 0, 2),
    ("W0", 0, 0), ("T0", 1, 2), ("T1", 1, 2), ("W1", 0, 0), ("W0", 1, 0), ("W1", 1, 0),
)


def kernel(
    tok_hbm, w_hbm, cot_hbm, act_hbm, own_hbm, other_hbm, gt_hbm,
    w, cot, act, tok, tok_t, part, f1, r1, s, f2, r2, g, gw, gwb, gt, zsend, zrecv,
    local_sem, out_sem, z_send, z_recv, send, g_send, f1_sem, r1_sem, f2_sem, r2_sem, g_sem,
    dep_send, dep_recv, zs_send, zs_recv,
):
    fh = g.shape[-1]
    half = 32
    depth, row, col = (lax.axis_index(a) for a in ("depth", "row", "col"))
    yx = (col // SIDE, col % SIDE)
    lo, hi = pl.ds(0, half), pl.ds(half, half)

    loads = [
        pltpu.make_async_copy(tok_hbm, tok.at[0, pl.ds(2 * row, 2)], local_sem.at[0]),
        pltpu.make_async_copy(w_hbm, w, local_sem.at[1]),
        pltpu.make_async_copy(cot_hbm, cot, local_sem.at[2]),
    ]
    for load in loads:
        load.start()

    def grid_device(axis, delta):
        at = list(yx)
        at[axis] = (at[axis] + delta + SIDE) % SIDE
        return {"col": at[0] * SIDE + at[1]}

    def row_device(delta):
        return {"row": (row + delta + ROWS) % ROWS}

    other = {"depth": 1 - depth}

    barrier = pltpu.get_barrier_semaphore()
    peers = [row_device(d) for d in range(1, ROWS)]
    peers += [grid_device(axis, delta) for axis in (0, 1) for delta in (1, 2, 3)]
    peers += [other]
    for peer in peers:
        pl.semaphore_signal(barrier, inc=1, device_id=peer, device_id_type=MESH)
    loads[0].wait()
    pl.semaphore_wait(barrier, len(peers))

    def remote(src, dst, ssem, rsem, device):
        return pltpu.make_async_remote_copy(
            src_ref=src, dst_ref=dst, send_sem=ssem, recv_sem=rsem,
            device_id=device, device_id_type=MESH,
        )

    def push(src, dst, ssem, rsem, device):
        remote(src, dst, ssem, rsem, device).start()

    def arrived(ref, rsem):
        remote(ref, ref, send.at[0, 0, 0], rsem, other).wait_recv()

    def sent(ref, ssem):
        remote(ref, ref, ssem, f2_sem.at[0, 0], other).wait_send()

    def piece(delta, k):
        return tok.at[0, 2 * ((row + delta + ROWS) % ROWS) + k]

    def hand_on(delta, k, way, far=1):
        sem = 4 * (abs(delta) + far - 1) + 2 * k + way
        device = row_device(far * (1 - 2 * way))
        push(piece(delta, k), piece(delta, k), z_send.at[sem], z_recv.at[sem], device)

    for k in (0, 1):
        hand_on(0, k, 0)
        hand_on(0, k, 1)
    gt[...] = jnp.zeros_like(gt)

    def task_z(step):
        for k in (0, 1):
            for way in (0, 1):
                if step == 4 and k != way:
                    continue
                delta = -step if way == 0 else step
                arrived(piece(delta, k), z_recv.at[4 * (step - 1) + 2 * k + way])
                if step < 3:
                    hand_on(delta, k, way)
                if step == 2 and k == way:
                    hand_on(delta, k, way, 2)

    def task_tokens():
        for at_y in range(SIDE):
            for at_x in range(SIDE):
                tok[1, at_x * SIDE + at_y] = tok[0, at_y * SIDE + at_x]

    def task_transposes():
        for h in range(2):
            for t in range(2):
                tok_t[h, t] = tok[h, :, pl.ds(32 * t, 32)].reshape(512, 384).T

    def ring(h):
        axis_a, axis_b = (1, 0) if h == 0 else (0, 1)
        return axis_a, axis_b, yx[axis_a], yx[axis_b]

    def slot(h, j, i):
        _, _, a, b = ring(h)
        return ((b + j) % SIDE) * SIDE + (a + i) % SIDE

    def columns(n, h):
        return pl.ds((2 * n + h) * fh, fh)

    def summed(n, h):
        width = part[n][h].shape[-1]
        return pl.ds(2 * n * fh + (0 if h == 0 else 2 * fh - width), width)

    def group(h, j):
        _, _, _, b = ring(h)
        return (b + j) % SIDE

    toward = 1 - 2 * (row % 2)
    waves = [row // 2, (row // 2 - toward + SIDE) % SIDE, (row // 2 + toward + SIDE) % SIDE, (row // 2 + 2) % SIDE]

    def first_sends(n, h, j):
        axis_a = ring(h)[0]
        right, left = grid_device(axis_a, 1), grid_device(axis_a, -1)
        ssem = send.at[n, h, 0]
        far = part[n][h].at[slot(h, j, 2)]
        push(far.at[lo], f1[n][h].at[j, 0], ssem, f1_sem.at[n, h, j, 0], right)
        push(far.at[hi], f1[n][h].at[j, 1], ssem, f1_sem.at[n, h, j, 1], left)
        push(part[n][h].at[slot(h, j, 1), hi], r1[n][h].at[j, 0, hi], ssem, r1_sem.at[n, h, j], right)
        push(part[n][h].at[slot(h, j, 3), lo], r1[n][h].at[j, 1, lo], ssem, r1_sem.at[n, h, j], left)

    def task_iw(n, wave):
        if wave == 0:
            loads[1].wait()
        at_y = waves[wave]
        role = (at_y - yx[0] + SIDE) % SIDE
        task_i(n, 0, role)
        x = tok[0, pl.ds(SIDE * at_y, SIDE)].reshape(256, 384)
        y = jnp.dot(x, w[:, summed(n, 1)], preferred_element_type=F32).astype(BF16)
        for at_x in range(SIDE):
            part[n][1][SIDE * at_x + at_y] = y[64 * at_x : 64 * at_x + 64]
        right, left = grid_device(0, 1), grid_device(0, -1)
        ssem = send.at[n, 1, 0]

        @pl.when(role == 2)
        def _():
            for j in range(SIDE):
                far = part[n][1].at[slot(1, j, 2)]
                push(far.at[lo], f1[n][1].at[j, 0], ssem, f1_sem.at[n, 1, j, 0], right)
                push(far.at[hi], f1[n][1].at[j, 1], ssem, f1_sem.at[n, 1, j, 1], left)

        @pl.when(role == 1)
        def _():
            for j in range(SIDE):
                push(part[n][1].at[slot(1, j, 1), hi], r1[n][1].at[j, 0, hi], ssem, r1_sem.at[n, 1, j], right)

        @pl.when(role == 3)
        def _():
            for j in range(SIDE):
                push(part[n][1].at[slot(1, j, 3), lo], r1[n][1].at[j, 1, lo], ssem, r1_sem.at[n, 1, j], left)

    def task_i(n, h, j):
        four = pl.ds(SIDE * group(h, j), SIDE)
        x = tok[h, four].reshape(256, 384)
        y = jnp.dot(x, w[:, summed(n, h)], preferred_element_type=F32).astype(BF16)
        part[n][h][four] = y.reshape(SIDE, 64, y.shape[-1])
        first_sends(n, h, j)

    def forward(n, h, j, way):
        axis_a = ring(h)[0]
        device = grid_device(axis_a, 1 - 2 * way)
        rows, near = (lo, 1) if way == 0 else (hi, 3)
        arrived(f1[n][h].at[j, way], f1_sem.at[n, h, j, way])
        f1[n][h][j, way] = (
            f1[n][h][j, way].astype(F32) + part[n][h][slot(h, j, near), rows].astype(F32)
        ).astype(BF16)
        push(f1[n][h].at[j, way], r1[n][h].at[j, way, rows], send.at[n, h, 1], r1_sem.at[n, h, j], device)

    def task_f(n, h, j):
        forward(n, h, j, 0)
        forward(n, h, j, 1)

    def sum_first(n, h, j):
        arrived(r1[n][h].at[j], r1_sem.at[n, h, j])
        total = part[n][h][slot(h, j, 0)].astype(F32)
        total = total + r1[n][h][j, 0].astype(F32) + r1[n][h][j, 1].astype(F32)
        s[n][h][j] = total.astype(BF16)

    def second_sends(n, h, j):
        axis_b = ring(h)[1]
        right, left = grid_device(axis_b, 1), grid_device(axis_b, -1)
        ssem = send.at[n, h, 2]
        if j == 2:
            push(s[n][h].at[2, lo], f2[n][h].at[0], ssem, f2_sem.at[n, h], right)
            push(s[n][h].at[2, hi], f2[n][h].at[1], ssem, f2_sem.at[n, h], left)
        elif j == 1:
            push(s[n][h].at[1, hi], r2[n][h].at[0, hi], ssem, r2_sem.at[n, h], right)
        elif j == 3:
            push(s[n][h].at[3, lo], r2[n][h].at[1, lo], ssem, r2_sem.at[n, h], left)

    def task_d(n, h, j):
        sum_first(n, h, j)
        second_sends(n, h, j)

    def task_dp(n, wave):
        j = (waves[wave] - yx[0] + SIDE) % SIDE
        sum_first(n, 0, j)
        for role in (1, 2, 3):
            pl.when(j == role)(functools.partial(second_sends, n, 0, role))

    def task_f2(n, h):
        axis_b = ring(h)[1]
        right, left = grid_device(axis_b, 1), grid_device(axis_b, -1)
        ssem = send.at[n, h, 2]
        arrived(f2[n][h], f2_sem.at[n, h])
        f2[n][h][0] = (f2[n][h][0].astype(F32) + s[n][h][1, lo].astype(F32)).astype(BF16)
        push(f2[n][h].at[0], r2[n][h].at[0, lo], ssem, r2_sem.at[n, h], right)
        f2[n][h][1] = (f2[n][h][1].astype(F32) + s[n][h][3, hi].astype(F32)).astype(BF16)
        push(f2[n][h].at[1], r2[n][h].at[1, hi], ssem, r2_sem.at[n, h], left)

    def task_d2(n, h):
        arrived(r2[n][h], r2_sem.at[n, h])

        @pl.loop(0, 4)
        def _(at):
            rows = pl.ds(pl.multiple_of(at * 16, 16), 16)
            hidden = s[n][h][0, rows].astype(F32) + r2[n][h][0, rows].astype(F32) + r2[n][h][1, rows].astype(F32)
            cdf, density = gelu_parts(hidden)
            act[rows, summed(n, h)] = (hidden * cdf).astype(BF16)
            grad = cot[rows, summed(n, h)].astype(F32) * (cdf + hidden * density)
            grad = grad.astype(BF16)
            width = grad.shape[-1]
            if h == 0:
                g[n, 0, slot(0, 0, 0), rows, 0 : min(width, fh)] = grad[:, 0 : min(width, fh)]
                if width > fh:
                    g[n, 1, slot(1, 0, 0), rows, 0 : width - fh] = grad[:, fh:width]
            else:
                g[n, 1, slot(1, 0, 0), rows, fh - width : fh] = grad

    def block(c, h, j, i):
        n, start, size, _ = GATHERS[c]
        return g.at[n, h, slot(h, j, i), pl.ds(start, size)]

    def share(c, h, j, i, axis, delta):
        n, start, size, straight = GATHERS[c]
        axis_a = ring(h)[0]
        nj, ni = (j, (i - delta) % SIDE) if axis == axis_a else ((j - delta) % SIDE, i)
        ref = block(c, h, j, i)
        if delta != 2 and 2 in (ni if axis == axis_a else nj,):
            ref = g.at[n, h, slot(h, j, i), pl.ds(start if delta == 1 else start + size // 2, size // 2)]
        push(ref, ref, g_send.at[c, h], g_sem.at[c, h, nj, ni], grid_device(axis, delta))

    def ways(c):
        return (1, -1, 2) if GATHERS[c][3] else (1, -1)

    here = set()

    def block_here(c, h, j, i):
        if (c, h, j, i) not in here:
            here.add((c, h, j, i))
            arrived(block(c, h, j, i), g_sem.at[c, h, j, i])

    def task_s(c, h):
        axis_a, axis_b, _, _ = ring(h)
        here.add((c, h, 0, 0))
        for axis in (axis_b, axis_a):
            for delta in ways(c):
                share(c, h, 0, 0, axis, delta)

    def task_a1(c, h):
        axis_a, axis_b, _, _ = ring(h)
        for j, delta in ((3, 1), (1, -1)):
            block_here(c, h, j, 0)
            if not GATHERS[c][3]:
                share(c, h, j, 0, axis_b, delta)
        for j in (3, 1):
            for delta in ways(c):
                share(c, h, j, 0, axis_a, delta)

    def task_a2(c, h):
        axis_a = ring(h)[0]
        block_here(c, h, 2, 0)
        for delta in ways(c):
            share(c, h, 2, 0, axis_a, delta)

    def task_a(c, h, step):
        if step == 1:
            task_a1(c, h)
        else:
            task_a2(c, h)

    def task_b(c, h, j):
        axis_a = ring(h)[0]
        if not GATHERS[c][3]:
            block_here(c, h, j, 3)
            share(c, h, j, 3, axis_a, 1)
            block_here(c, h, j, 1)
            share(c, h, j, 1, axis_a, -1)

    finished = set()

    def task_t(c, h, i):
        n, start, size, _ = GATHERS[c]
        rows = pl.ds(start, size)
        at_x = (yx[1] + i) % SIDE
        for k in range(SIDE):
            block_here(c, h, *((k, i) if h == 0 else (i, k)))
        if h == 0:
            blocks = jnp.concatenate([g[n, h, SIDE * at_y + at_x, rows] for at_y in range(SIDE)], axis=0)
        else:
            blocks = g[n, h, pl.ds(SIDE * at_x, SIDE), rows].reshape(SIDE * size, fh)
        terms = lax.dot_general(
            blocks, w[:, columns(n, h)], (((1,), (1,)), ((), ())), preferred_element_type=F32
        )
        for at_y in range(SIDE):
            at = SIDE * at_y + at_x
            gt[at, rows] = gt[at, rows] + terms[size * at_y : size * at_y + size]
        finished.add((c, h, i))
        if n == NCH - 1 and (c, 1 - h, i) in finished:
            for at_y in range(SIDE):
                send_tokens(SIDE * at_y + at_x, rows)

    def send_tokens(at, rows):
        zsend[at, rows] = gt[at, rows].astype(BF16)
        to = at // 2
        ahead = (to - row + ROWS) % ROWS

        @pl.when(ahead != 0)
        def _():
            place = ROWS - 1 - ahead
            push(zsend.at[at, rows], zrecv.at[place, at % 2, rows], zs_send.at[0], zs_recv.at[0], {"row": to})

    def task_w(c, h):
        n, start, size, _ = GATHERS[c]
        for j in range(SIDE):
            for i in range(SIDE):
                block_here(c, h, j, i)
        total = None
        for t in range(start // half, (start + size) // half):
            rows = g[n, h, :, pl.ds(half * t, half)].reshape(512, fh)
            term = jnp.dot(tok_t[h, t], rows, preferred_element_type=F32)
            total = term if total is None else total + term
        if start > 0:
            total = gw[n, h] + total
        if start + size < 64:
            gw[n, h] = total
        else:
            gwb[n, h] = total.astype(BF16)
            cols = columns(n, h)
            push(gwb.at[n, h], other_hbm.at[:, cols], dep_send.at[n, h], dep_recv.at[n, h], other)
            pltpu.make_async_copy(gwb.at[n, h], own_hbm.at[:, cols], out_sem.at[n, h]).start()

    by_half = {
        "I": task_i, "F": task_f, "D": task_d, "G": task_f2, "H": task_d2,
        "S": task_s, "A": task_a, "B": task_b, "T": task_t, "W": task_w,
    }
    without_step = "GHSW"
    act_out = pltpu.make_async_copy(act, act_hbm, local_sem.at[0])
    halves_done = 0
    cot_waited = False
    for name, n, j in ORDER:
        if name[0] == "H" and not cot_waited:
            loads[2].wait()
            cot_waited = True
        if name == "Z":
            task_z(j)
        elif name == "IW":
            task_iw(n, j)
        elif name == "FP":
            task_f(n, 0, (waves[j] - yx[0] + SIDE) % SIDE)
        elif name == "FQ":
            for k in range(SIDE):
                forward(n, 1, k, j)
        elif name == "DP":
            task_dp(n, j)
        elif name == "tokens":
            task_tokens()
        elif name == "transposes":
            task_transposes()
        elif name[0] in without_step:
            by_half[name[0]](n, int(name[1]))
            halves_done += name[0] == "H"
            if name[0] == "H" and halves_done == 2 * NCH:
                act_out.start()
        else:
            by_half[name[0]](n, int(name[1]), j)

    for n in range(NCH):
        for h in (0, 1):
            sent(r1[n][h], send.at[n, h, 0])
            sent(s[n][h], send.at[n, h, 1])
            sent(s[n][h].at[pl.ds(0, 3)], send.at[n, h, 2])
    for c, (n, start, size, _) in enumerate(GATHERS):
        for h in (0, 1):
            sent(g.at[n, h, pl.ds(0, 15), pl.ds(start, size)], g_send.at[c, h])
    for delta in range(4):
        for k in (0, 1):
            for way in (0, 1):
                if delta < 3 or k == way:
                    sent(tok.at[0, 0], z_send.at[4 * delta + 2 * k + way])
    arrived(zrecv, zs_recv.at[0])
    for at in range(2):
        total = gt[2 * row + at].astype(BF16).astype(F32)
        for place in range(ROWS - 1):
            total = total + zrecv[place, at].astype(F32)
        zsend[2 * row + at] = total.astype(BF16)
    gt_out = pltpu.make_async_copy(zsend.at[pl.ds(2 * row, 2)], gt_hbm, local_sem.at[1])
    gt_out.start()

    for n in range(NCH):
        for h in (0, 1):
            cols = columns(n, h)
            pltpu.make_async_copy(gwb.at[n, h], own_hbm.at[:, cols], out_sem.at[n, h]).wait()
            done = remote(gwb.at[n, h], other_hbm.at[:, cols], dep_send.at[n, h], dep_recv.at[n, h], other)
            done.wait_send()
            done.wait_recv()
    sent(zsend.at[pl.ds(0, 14)], zs_send.at[0])
    act_out.wait()
    gt_out.wait()


def finish(own, other, act, gt, gw_out, act_out, gt_out, total, sem):
    copies = [pltpu.make_async_copy(act, act_out, sem.at[6]), pltpu.make_async_copy(gt, gt_out, sem.at[7])]
    for copy in copies:
        copy.start()
    step = own.shape[0] // 6
    for k in range(6):
        rows = pl.ds(k * step, step)
        total[rows] = (own[rows].astype(F32) + other[rows].astype(F32)).astype(BF16)
        copies.append(pltpu.make_async_copy(total.at[rows], gw_out.at[rows], sem.at[k]))
        copies[-1].start()
    for copy in copies:
        copy.wait()


def local(tokens, weight, cotangent):
    d, f = weight.shape
    fh = f // (2 * NCH)
    any_spec = pl.BlockSpec(memory_space=pl.ANY)
    vmem = pltpu.VMEM
    dma = pltpu.SemaphoreType.DMA

    def halves(*shape):
        return tuple(
            tuple(vmem(shape + (2 * fh * part // 12,), BF16) for part in (share, 12 - share)) for share in X_FIRST
        )

    act, own, other, gt = pl.pallas_call(
        kernel,
        out_shape=(
            jax.ShapeDtypeStruct(cotangent.shape, BF16),
            jax.ShapeDtypeStruct(weight.shape, BF16),
            jax.ShapeDtypeStruct(weight.shape, BF16),
            jax.ShapeDtypeStruct((2, 64, d), BF16),
        ),
        in_specs=[any_spec] * 3,
        out_specs=(any_spec,) * 4,
        scratch_shapes=[
            vmem(weight.shape, BF16),
            vmem(cotangent.shape, BF16),
            vmem(cotangent.shape, BF16),
            vmem((2, 16, 64, d), BF16),
            vmem((2, 2, d, 512), BF16),
            halves(16, 64),
            halves(SIDE, 2, 32),
            halves(SIDE, 2, 64),
            halves(SIDE, 64),
            halves(2, 32),
            halves(2, 64),
            vmem((NCH, 2, 16, 64, fh), BF16),
            vmem((NCH, 2, d, fh), F32),
            vmem((NCH, 2, d, fh), BF16),
            vmem((16, 64, d), F32),
            vmem((16, 64, d), BF16),
            vmem((ROWS - 1, 2, 64, d), BF16),
            dma((3,)),
            dma((NCH, 2)),
            dma((16,)),
            dma((16,)),
            dma((NCH, 2, 3)),
            dma((len(GATHERS), 2)),
            dma((NCH, 2, SIDE, 2)),
            dma((NCH, 2, SIDE)),
            dma((NCH, 2)),
            dma((NCH, 2)),
            dma((len(GATHERS), 2, SIDE, SIDE)),
            dma((NCH, 2)),
            dma((NCH, 2)),
            dma((1,)),
            dma((1,)),
        ],
        compiler_params=pltpu.CompilerParams(
            collective_id=0, has_side_effects=True, vmem_limit_bytes=48 * 2**20
        ),
    )(tokens.reshape(2, 64, d), weight, cotangent)
    grad_weight, act, gt = pl.pallas_call(
        finish,
        out_shape=(
            jax.ShapeDtypeStruct(weight.shape, BF16),
            jax.ShapeDtypeStruct(cotangent.shape, BF16),
            jax.ShapeDtypeStruct((2, 64, d), BF16),
        ),
        in_specs=[pl.BlockSpec(memory_space=vmem)] * 4,
        out_specs=(pl.BlockSpec(memory_space=pltpu.HBM),) * 3,
        scratch_shapes=[vmem(weight.shape, BF16), dma((8,))],
        compiler_params=pltpu.CompilerParams(vmem_limit_bytes=8 * 2**20),
    )(own, other, act, gt)
    return (act, gt.reshape(128, d), grad_weight)


def solution(mesh):
    placed = (P(("depth", "row"), "col"), P("col", "row"), P(("depth", "col"), "row"))
    return jax.shard_map(
        local,
        mesh=mesh,
        in_specs=placed,
        out_specs=(P(("depth", "col"), "row"), P(("depth", "row"), "col"), P("col", "row")),
        check_vma=False,
    )
```
